128 devices in a mesh: axial: 8 (over y, x_hi), azim: 16 (over x_lo, z, core).
Axes of the slice: x: 4 (x_hi: 2, x_lo: 2; x = x_hi * 2 + x_lo), y: 4, z: 4, core: 2. Of those that a mesh axis runs over, the one named last changes fastest.
Arguments:
- positions: float32 [8, 16, 32, 3, 128], P('axial', 'azim'), may hold values from 0 to 1, as said below
- velocities: float32 [8, 16, 32, 3, 128], P('axial', 'azim'), may hold values from -6 to 6
- radius: float32 [8, 16, 32, 128], P('axial', 'azim'), may hold values from 0.04 to 0.07
- gas_velocity: float32 [8, 16, 32, 3, 128], P('axial', 'azim'), may hold values from -8 to 8
- history: float32 [8, 16, 64, 3, 128, 128], P('axial', 'azim'), may hold values from -0.12 to 0.12
- pair_list: int32 [8, 16, 2, 64], P('axial', 'azim'), may hold values from 0 to 127, as said below
- history_slot: int32 [8, 16, 64], P('axial', 'azim'), may hold values from 0 to 63, each once within a row
- pair_count: int32 [8, 16], P('axial', 'azim'), may hold values from 4 to 64, as said below
- new_home: int32 [8, 16, 32], P('axial', 'azim'), may hold values from 0 to 4095, as said below
Outputs:
- moved_positions: float32 [8, 16, 32, 3, 128], P('axial', 'azim')
- moved_velocities: float32 [8, 16, 32, 3, 128], P('axial', 'azim')
- moved_radius: float32 [8, 16, 32, 128], P('axial', 'azim')
- history_out: float32 [8, 16, 64, 3, 128, 128], P('axial', 'azim')
The draws below stay inside these ranges and needn't reach their ends.
Inputs may be any that keep to these rules, and one draw needn't show every extreme that they name: `positions`: each block's particles lie within 0.3 of its cell centre in every component; cell centres lie in 0.3 to 0.7. `pair_list`: row 0 names an own block, below 32; row 1 a block of the extended blocks, below 128; an own partner has a larger number than the first block; no unordered pair appears twice in a device's list; devices of the last section name no partner of a following section. `history_slot`: each device's slots are distinct. `pair_count`: A multiple of 4; the pairs from this place on in a device's list are inactive. `new_home`: A permutation of all places; every device keeps exactly 8 of its blocks and sends exactly 8 blocks to each of three other devices, which may lie anywhere in the pipe.
All inputs are finite; a program needn't handle non-finite values.
Results may differ from the reference program's by a relative error of at most 0.0003.
Values sent between devices are 32-bit elements; how exact they have to be, the bound alone decides.
A program may use at most 128 MiB of HBM per device.

```python
import math
import jax
import jax.numpy as jnp
from jax import lax

PB = 128
BLK = 32
PAIRS = 64
ITERS = 3
SECTIONS = 8
SECTORS = 16


def draw_positions(key, part):
    key = jax.random.fold_in(key, 10)
    first, second = jax.random.split(key, 2)
    centre = jax.random.uniform(first, (SECTIONS, SECTORS, BLK, 3, 1), jnp.float32, 0.3, 0.7)
    offset = jax.random.uniform(second, (SECTIONS, SECTORS, BLK, 3, PB), jnp.float32, -0.3, 0.3)
    return (centre + offset).astype(jnp.float32)


def draw_pair_list(key, part):
    key = jax.random.fold_in(key, 11)
    codes = BLK * 4 * BLK

    def one_device(device):
        sub = jax.random.fold_in(key, device)
        shuffle = jax.random.permutation(sub, codes)
        code = jnp.arange(codes, dtype=jnp.int32)
        first = code // (4 * BLK)
        second = code % (4 * BLK)
        region = second // BLK
        last = device // SECTORS == SECTIONS - 1
        cross_ok = jnp.where(region == 2, True, jnp.logical_not(last))
        valid = jnp.where(region == 0, second > first, cross_ok)
        score = jnp.where(valid, 0, codes) + shuffle
        chosen = jnp.argsort(score)[:PAIRS]
        return jnp.stack([first[chosen], second[chosen]])
    result = jax.vmap(one_device)(jnp.arange(SECTIONS * SECTORS, dtype=jnp.int32))
    return result.reshape(SECTIONS, SECTORS, 2, PAIRS).astype(jnp.int32)


def draw_pair_count(key, part):
    key = jax.random.fold_in(key, 12)
    groups = PAIRS // 4
    first, second = jax.random.split(key, 2)
    lower = jnp.minimum(jax.random.randint(first, (SECTIONS, SECTORS), 0, groups), jax.random.randint(second, (SECTIONS, SECTORS), 0, groups))
    counted = 4 * (1 + lower)
    return counted.at[0, 0].set(PAIRS).astype(jnp.int32)


def draw_new_home(key, part):
    key = jax.random.fold_in(key, 13)
    capacity = BLK // 4
    devices = SECTIONS * SECTORS
    half = devices // 2
    first, third = jax.random.split(key, 2)
    far_shift = jax.random.randint(first, (), 2, half).astype(jnp.int32)
    keys = jax.random.split(third, devices)
    shuffled = jax.vmap(lambda sub: jax.random.permutation(sub, BLK))(keys).reshape(SECTIONS, SECTORS, BLK)
    group = shuffled // capacity
    zero = jnp.zeros((), jnp.int32)
    shift_table = jnp.stack([zero, zero + 1, zero + half, far_shift])
    section = jnp.arange(SECTIONS, dtype=jnp.int32)[:, None, None]
    sector = jnp.arange(SECTORS, dtype=jnp.int32)[None, :, None]
    flat = section * SECTORS + sector
    target = (flat + shift_table[group]) % devices
    return (target * BLK + shuffled).astype(jnp.int32)


def steps_of(stream_key, extent, pieces, low, largest):
    def one(dim, shards_of):
        heights = jax.random.uniform(jax.random.fold_in(jax.random.fold_in(stream_key, 6), dim), (shards_of,), jnp.float32, low / len(pieces), largest / len(pieces))
        return jnp.repeat(jnp.exp(heights), extent[dim] // shards_of).reshape((-1,) + (1,) * (len(extent) - dim - 1))

    gain = one(*pieces[0])
    for cut in pieces[1:]:
        gain = gain * one(*cut)
    return gain


def normal_values(rng, shape, scale, most, cuts=(), kind=jnp.bfloat16):
    values = scale * jax.random.normal(rng, shape, jnp.float32)
    if cuts:
        values = values * steps_of(rng, shape, cuts, -0.22, 0.18)
    return jnp.clip(values, -most, most).astype(kind)


def setup_inputs(seed: int = 0) -> dict:
    seeds = jax.random.split(jax.random.key(seed), 10)
    positions = draw_positions(jax.random.fold_in(seeds[9], 71), 0)
    velocities = normal_values(seeds[1], (SECTIONS, SECTORS, BLK, 3, PB), 1.0, 6.0, ((0, 8), (1, 16)), jnp.float32)
    radius = jnp.clip(jnp.exp(math.log(0.07) - 0.5596158 * jax.random.uniform(seeds[2], (SECTIONS, SECTORS, BLK, PB), jnp.float32) ** steps_of(seeds[2], (SECTIONS, SECTORS, BLK, PB), ((0, 8), (1, 16)), -0.2, 0.2)), 0.04, 0.07)
    gas_velocity = normal_values(seeds[3], (SECTIONS, SECTORS, BLK, 3, PB), 2.0, 8.0, ((0, 8), (1, 16)), jnp.float32)
    history = normal_values(seeds[4], (SECTIONS, SECTORS, PAIRS, 3, PB, PB), 0.02, 0.12, ((0, 8), (1, 16)), jnp.float32)
    pair_list = draw_pair_list(jax.random.fold_in(seeds[9], 71), 0)
    history_slot = jax.vmap(lambda own: jax.random.permutation(own, PAIRS))(jax.random.split(seeds[6], SECTIONS * SECTORS)).reshape((SECTIONS, SECTORS, PAIRS)).astype(jnp.int32)
    pair_count = draw_pair_count(jax.random.fold_in(seeds[9], 71), 0)
    new_home = draw_new_home(jax.random.fold_in(seeds[9], 71), 0)
    return dict(positions=positions, velocities=velocities, radius=radius, gas_velocity=gas_velocity, history=history, pair_list=pair_list, history_slot=history_slot, pair_count=pair_count, new_home=new_home)


STIFF_NORMAL = 10000.0
STIFF_TANGENT = 8000.0
DAMP_NORMAL = 40.0
STEP_TIME = 0.01
DRAG_TIME = 0.05
FADE_DEPTH = 0.01
GAP_FLOOR = 0.01
MASS_RADIUS = 0.06
GRAVITY_PULL = -9.81

def contact(near, far, memory):
    apart = near[:, 0:3, :, None] - far[:, 0:3, None, :]
    dist = jnp.sqrt(lax.optimization_barrier(jnp.sum(apart * apart, axis=1)))
    over = jnp.maximum(near[:, 6, :, None] + far[:, 6, None, :] - dist, 0.0)
    root = jnp.sqrt(over)
    normal = apart / jnp.maximum(dist, GAP_FLOOR)[:, None]
    relative = near[:, 3:6, :, None] - far[:, 3:6, None, :]
    along = lax.optimization_barrier(jnp.sum(relative * normal, axis=1))
    tangent = relative - along[:, None] * normal
    fade = jnp.minimum(over / FADE_DEPTH, 1.0)
    fresh = fade[:, None] * (memory + STEP_TIME * tangent)
    magnitude = STIFF_NORMAL * over * root - DAMP_NORMAL * root * along
    force = magnitude[:, None] * normal - STIFF_TANGENT * root[:, None] * fresh
    return (lax.optimization_barrier(jnp.sum(force, axis=3)), -lax.optimization_barrier(jnp.sum(force, axis=2)), fresh)

def next_section(field):
    return jnp.concatenate([field[1:], jnp.zeros_like(field[:1])], axis=0)

def prior_section(field):
    return jnp.concatenate([jnp.zeros_like(field[:1]), field[:-1]], axis=0)

def reference(positions, velocities, radius, gas_velocity, history, pair_list, history_slot, pair_count, new_home):
    devices = SECTIONS * SECTORS
    place = positions
    speed = velocities
    memory = history.reshape(devices, PAIRS, 3, PB, PB)
    pairs = pair_list.reshape(devices, 2, PAIRS)
    slots = history_slot.reshape(devices, PAIRS)
    counts = pair_count.reshape(devices)
    mass = (radius / MASS_RADIUS) ** 3
    gravity = jnp.array([0.0, GRAVITY_PULL, 0.0], jnp.float32).reshape(1, 1, 1, 3, 1)

    def device_work(inputs):
        blocks, pair_rows, slot_row, count, kept = inputs
        active = jnp.arange(PAIRS) < count
        old = kept[slot_row]
        f_near, f_far, fresh = contact(blocks[pair_rows[0]], blocks[pair_rows[1]], old)
        weight = active.astype(f_near.dtype)[:, None, None]
        acting = jnp.zeros((4 * BLK, 3, PB), f_near.dtype)
        acting = acting.at[pair_rows[0]].add(f_near * weight).at[pair_rows[1]].add(f_far * weight)
        fresh = jnp.where(active[:, None, None, None], fresh, old)
        return (acting, kept.at[slot_row].set(fresh))
    for substep in range(ITERS):
        state = jnp.concatenate([place, speed, radius[:, :, :, None, :]], axis=3)
        sector_next = jnp.roll(state, -1, axis=1)
        extended = jnp.concatenate([state, next_section(state), sector_next, next_section(sector_next)], axis=2)
        extended = extended.reshape(devices, 4 * BLK, 7, PB)
        acting, memory = lax.map(device_work, (extended, pairs, slots, counts, memory))
        acting = acting.reshape(SECTIONS, SECTORS, 4, BLK, 3, PB)
        total = acting[:, :, 0] + prior_section(acting[:, :, 1]) + jnp.roll(acting[:, :, 2], 1, axis=1)
        total = total + prior_section(jnp.roll(acting[:, :, 3], 1, axis=1))
        accel = total / mass[:, :, :, None, :] + gravity + (gas_velocity - speed) / DRAG_TIME
        speed = speed + STEP_TIME * accel
        place = place + STEP_TIME * speed
    state = jnp.concatenate([place, speed, radius[:, :, :, None, :]], axis=3).reshape(devices * BLK, 7, PB)
    moved = jnp.zeros_like(state).at[new_home.reshape(-1)].set(state)
    moved = moved.reshape(SECTIONS, SECTORS, BLK, 7, PB)
    return (moved[:, :, :, 0:3], moved[:, :, :, 3:6], moved[:, :, :, 6], memory.reshape(SECTIONS, SECTORS, PAIRS, 3, PB, PB))
```

```python
import functools
import jax
import jax.numpy as jnp
from jax import lax
from jax.experimental import pallas as pl
from jax.experimental.pallas import tpu as pltpu
from jax.sharding import PartitionSpec as P

ITERS = 3
BLK = 32
PAIRS = 64
PB = 128
GROUP = 8
STEP_TIME = 0.01
GRAVITY_PULL = -9.81
MESH = pl.DeviceIdType.MESH
F32 = jnp.float32
BF16 = jnp.bfloat16


def split3(value):
    hi = value.astype(BF16)
    rest = value - hi.astype(F32)
    mid = rest.astype(BF16)
    lo = (rest - mid.astype(F32)).astype(BF16)
    return hi, mid, lo


def exact_dot(onehot, value):
    out = None
    for part in split3(value):
        term = jnp.dot(onehot, part, preferred_element_type=F32)
        out = term if out is None else out + term
    return out


def pair_body(codes, ext, near_bc, hist, pairs_f, slot):
    code = codes[slot]
    a = code // 256
    c = code % 256
    lane = lax.broadcasted_iota(jnp.int32, (8, PB), 1)
    sub = lax.broadcasted_iota(jnp.int32, (8, PB), 0)
    bits = [(lane & (1 << level)) == 0 for level in range(4)]
    far = [jnp.broadcast_to(ext[q, pl.ds(c, 1), :], (8, PB)) for q in range(7)]
    column = [None] * 3
    waiting = [[None] * 4 for _ in range(3)]
    rows = [None] * 3

    def merge(t, level, value):
        while level < 4:
            if waiting[t][level] is None:
                waiting[t][level] = value
                return
            first = waiting[t][level]
            waiting[t][level] = None
            kept = jnp.where(bits[level], first, value)
            moved = jnp.where(bits[level], value, first)
            value = kept + pltpu.roll(moved, PB - (1 << level), 1)
            level += 1
        for level in range(4, 7):
            value = value + pltpu.roll(value, PB - (1 << level), 1)
        rows[t] = value

    for k in range(16):
        r = slice(8 * k, 8 * k + 8)
        near = [near_bc[a, q, r, :] for q in range(7)]
        d = [near[q] - far[q] for q in range(3)]
        w = [near[q] - far[q] for q in range(3, 6)]
        d2 = jnp.maximum(d[0] * d[0] + d[1] * d[1] + d[2] * d[2], 1e-30)
        rs = lax.rsqrt(d2)
        inv = jnp.minimum(rs, 1.0)
        over = jnp.maximum(near[6] + far[6] - d2 * rs, 0.0)
        root = over * lax.rsqrt(jnp.maximum(over, 1e-30))
        q = (w[0] * d[0] + w[1] * d[1] + w[2] * d[2]) * (inv * inv)
        fade = jnp.minimum(over, 1.0)
        pull = root * (over * inv - 40.0 * q)
        drag = 80.0 * root
        for t in range(3):
            fresh = fade * (hist[slot, t, r, :] + (w[t] - q * d[t]))
            hist[slot, t, r, :] = fresh
            force = pull * d[t] - drag * fresh
            column[t] = force if column[t] is None else column[t] + force
            merge(t, 0, force)
    for t in range(3):
        pairs_f[t, pl.ds(PAIRS + slot, 1), :] = jnp.sum(column[t], axis=0, keepdims=True)
        picked = jnp.where(lane // 16 == sub, rows[t], 0.0)
        pairs_f[t, pl.ds(slot, 1), :] = jnp.sum(picked, axis=0, keepdims=True)


def kernel(sections, sectors, codes, targets, pos, vel, rad, gas, history,
           x_out, v_out, hist_out,
           ext, near_bc, hist, turned, pairs_f, acting, back, x_own, v_own,
           hist_in_sem, hist_out_sem, first_send, first_recv, halo_send, halo_recv, back_send, back_recv):
    i = lax.axis_index("axial")
    j = lax.axis_index("azim")
    up = lax.rem(i + 1, sections)
    down = lax.rem(i + sections - 1, sections)
    right = lax.rem(j + 1, sectors)
    left = lax.rem(j + sectors - 1, sectors)
    before = [(down, j), (i, left), (down, left)]
    after = [(up, j), (i, right), (up, right)]

    load = pltpu.make_async_copy(history, hist, hist_in_sem)
    load.start()
    barrier = pltpu.get_barrier_semaphore()
    for peer in before + after:
        pl.semaphore_signal(barrier, inc=1, device_id=peer, device_id_type=MESH)

    for t in range(3):
        x = pos[:, t, :]
        v = vel[:, t, :]
        x_own[t] = x
        v_own[t] = v
        ext[t, 0:BLK, :] = 100.0 * x
        ext[3 + t, 0:BLK, :] = STEP_TIME * v
    ext[6, 0:BLK, :] = 100.0 * rad[...]
    for q in range(7):
        idle = 100.0 if q == 6 else 0.0
        ext[q, 4 * BLK:4 * BLK + 8, :] = jnp.full((8, PB), idle, F32)
        near_bc[BLK, q] = jnp.full((PB, PB), idle, F32)
    pl.semaphore_wait(barrier, 6)

    def send(planes, sends, recvs):
        copies = []
        for n in range(3):
            copies.append(pltpu.make_async_remote_copy(
                src_ref=ext.at[planes, 0:BLK, :],
                dst_ref=ext.at[planes, (n + 1) * BLK:(n + 2) * BLK, :],
                send_sem=sends.at[n], recv_sem=recvs.at[n],
                device_id=before[n], device_id_type=MESH))
            copies[-1].start()
        return copies

    def spread(q_from, q_to):
        def one(k, _):
            r = pl.ds(pl.multiple_of(8 * k, 8), 8)
            for q in range(q_from, q_to):
                tile = turned[q // 4, r, :]
                for a in range(BLK):
                    lane_at = (q % 4) * BLK + a
                    near_bc[a, q, r, :] = jnp.broadcast_to(tile[:, lane_at:lane_at + 1], (8, PB))
            return 0
        lax.fori_loop(0, 16, one, 0)

    def turn():
        low = jnp.concatenate([ext[q, 0:BLK, :] for q in range(4)], axis=0)
        high = jnp.concatenate([ext[q, 0:BLK, :] for q in range(4, 7)] + [jnp.zeros((BLK, PB), F32)], axis=0)
        turned[0] = jnp.transpose(low)
        turned[1] = jnp.transpose(high)

    lane = lax.broadcasted_iota(jnp.int32, (PAIRS, PB), 1)
    home_lane = (lane % 8) * 16 + lane // 8
    block = lax.broadcasted_iota(jnp.int32, (4 * BLK, PB), 0)
    onehot = (jnp.broadcast_to(targets[...], (4 * BLK, PB)) == block).astype(F32)
    onehot = jnp.where(lax.broadcasted_iota(jnp.int32, (4 * BLK, PB), 1) < PAIRS, onehot, -onehot).astype(BF16)
    mass = rad[...] / 0.06
    mass = mass * mass * mass

    stores = []
    for substep in range(ITERS):
        if substep == 0:
            copies = send(slice(0, 7), first_send, first_recv)
        else:
            copies = send(slice(3, 6), halo_send, halo_recv)
        turn()
        spread(0, 7 if substep == 0 else 6)
        for copy in copies:
            copy.wait()
        if substep == 0:
            load.wait()
        else:
            for t in range(3):
                ext[t, BLK:4 * BLK, :] = ext[t, BLK:4 * BLK, :] + 100.0 * ext[3 + t, BLK:4 * BLK, :]

        def one_group(g, _):
            def one_pair(p, _):
                pair_body(codes, ext, near_bc, hist, pairs_f, g * GROUP + p)
                return 0
            lax.fori_loop(0, GROUP, one_pair, 0)
            if substep == ITERS - 1:
                pltpu.make_async_copy(hist.at[pl.ds(g * GROUP, GROUP)], hist_out.at[pl.ds(g * GROUP, GROUP)],
                                      hist_out_sem.at[g]).start()
            return 0

        lax.fori_loop(0, PAIRS // GROUP, one_group, 0)

        for t in range(3):
            near_rows = jnp.take_along_axis(pairs_f[t, 0:PAIRS, :], home_lane, axis=1, mode="promise_in_bounds")
            both = jnp.concatenate([near_rows, pairs_f[t, PAIRS:, :]], axis=0)
            acting[t] = exact_dot(onehot, both)
        returns = []
        for n in range(3):
            returns.append(pltpu.make_async_remote_copy(
                src_ref=acting.at[:, (n + 1) * BLK:(n + 2) * BLK, :],
                dst_ref=back.at[n],
                send_sem=back_send.at[n], recv_sem=back_recv.at[n],
                device_id=after[n], device_id_type=MESH))
            returns[-1].start()
        for copy in returns:
            copy.wait()
        for t in range(3):
            total = (acting[t, 0:BLK, :] + back[0, t] + back[1, t] + back[2, t]) * 10.0
            v = v_own[t]
            accel = total / mass + (gas[:, t, :] - v) / 0.05
            if t == 1:
                accel = accel + GRAVITY_PULL
            v = v + STEP_TIME * accel
            x = x_own[t] + STEP_TIME * v
            v_own[t] = v
            x_own[t] = x
            ext[t, 0:BLK, :] = 100.0 * x
            ext[3 + t, 0:BLK, :] = STEP_TIME * v
    x_out[...] = x_own[...]
    v_out[...] = v_own[...]

    def drain(g, _):
        pltpu.make_async_copy(hist.at[pl.ds(g * GROUP, GROUP)], hist_out.at[pl.ds(g * GROUP, GROUP)],
                              hist_out_sem.at[g]).wait()
        return 0
    lax.fori_loop(0, PAIRS // GROUP, drain, 0)


def substeps(sections, sectors, codes, targets, pos, vel, rad, gas, history):
    vmem = pl.BlockSpec(memory_space=pltpu.VMEM)
    plane = jax.ShapeDtypeStruct((3, BLK, PB), F32)
    return pl.pallas_call(
        functools.partial(kernel, sections, sectors),
        out_shape=(plane, plane, jax.ShapeDtypeStruct(history.shape, F32)),
        in_specs=[pl.BlockSpec(memory_space=pltpu.SMEM)] + [vmem] * 5 + [pl.BlockSpec(memory_space=pl.ANY)],
        out_specs=(vmem, vmem, pl.BlockSpec(memory_space=pl.ANY)),
        scratch_shapes=[
            pltpu.VMEM((7, 4 * BLK + 8, PB), F32),
            pltpu.VMEM((BLK + 1, 7, PB, PB), F32),
            pltpu.VMEM((PAIRS, 3, PB, PB), F32),
            pltpu.VMEM((2, PB, PB), F32),
            pltpu.VMEM((3, 2 * PAIRS, PB), F32),
            pltpu.VMEM((3, 4 * BLK, PB), F32),
            pltpu.VMEM((3, 3, BLK, PB), F32),
            pltpu.VMEM((3, BLK, PB), F32),
            pltpu.VMEM((3, BLK, PB), F32),
            pltpu.SemaphoreType.DMA,
            pltpu.SemaphoreType.DMA((PAIRS // GROUP,)),
            pltpu.SemaphoreType.DMA((3,)),
            pltpu.SemaphoreType.DMA((3,)),
            pltpu.SemaphoreType.DMA((3,)),
            pltpu.SemaphoreType.DMA((3,)),
            pltpu.SemaphoreType.DMA((3,)),
            pltpu.SemaphoreType.DMA((3,)),
        ],
        compiler_params=pltpu.CompilerParams(collective_id=0, has_side_effects=True, vmem_limit_bytes=48 << 20),
        name="substeps",
    )(codes, targets, pos, vel, rad, gas, history)


def aimed(target, slot, toward, order):
    return ((target == toward)[None, :] & (slot[None, :] == order[:, None])).astype(jnp.float32)


def local(
    positions,
    velocities,
    radius,
    gas_velocity,
    history,
    pair_list,
    history_slot,
    pair_count,
    new_home,
):
    radii = radius[0, 0]
    blocks, width = radii.shape
    order = jnp.arange(PAIRS, dtype=jnp.int32)
    chosen = (history_slot[0, 0][None, :] == order[:, None]) & (order < pair_count[0, 0])[None, :]
    idle = BLK * 256 + 4 * BLK
    code = pair_list[0, 0, 0] * 256 + pair_list[0, 0, 1] - idle
    codes = idle + jnp.sum(jnp.where(chosen, code[None, :], 0), axis=1)
    near = jnp.where(codes == idle, 4 * BLK, codes // 256)
    targets = jnp.concatenate([near, codes % 256])[None, :]
    place, speed, memory = substeps(
        lax.axis_size("axial"), lax.axis_size("azim"), codes, targets,
        positions[0, 0], velocities[0, 0], radii, gas_velocity[0, 0], history[0, 0])
    place = jnp.transpose(place, (1, 0, 2))
    speed = jnp.transpose(speed, (1, 0, 2))
    rows = jnp.concatenate([place, speed, radii[:, None, :]], axis=1).reshape(blocks, 7 * width)
    home = new_home[0, 0]
    target = home // blocks
    slot = home % blocks
    sections = lax.axis_size("axial")
    sectors = lax.axis_size("azim")
    here_axial = lax.axis_index("axial")
    here_azim = lax.axis_index("azim")
    myself = here_axial * sectors + here_azim
    order = jnp.arange(blocks, dtype=jnp.int32)
    settled = jnp.dot(aimed(target, slot, myself, order), rows, precision=lax.Precision.HIGHEST)
    devices = sections * sectors
    capacity = blocks // 4
    earlier = (target[None, :] == target[:, None]) & (order[None, :] < order[:, None])
    rank = jnp.sum(earlier.astype(jnp.int32), axis=1)
    leaving = target != myself
    select = (
        leaving[None, None, :]
        & (target[None, None, :] == jnp.arange(devices, dtype=jnp.int32)[:, None, None])
        & (rank[None, None, :] == jnp.arange(capacity, dtype=jnp.int32)[None, :, None])
    ).astype(jnp.float32)
    packed = jnp.einsum("dcb,bf->dcf", select, rows, precision=lax.Precision.HIGHEST)
    labels = jnp.sum(select * (slot + 1).astype(jnp.float32)[None, None, :], axis=2)
    arrived, arrived_labels = (
        lax.all_to_all(packed, ("axial", "azim"), split_axis=0, concat_axis=0, tiled=True),
        lax.all_to_all(labels, ("axial", "azim"), split_axis=0, concat_axis=0, tiled=True),
    )
    fitting = (
        arrived_labels.reshape(-1)[None, :] == (order[:, None] + 1).astype(jnp.float32)
    ).astype(jnp.float32)
    settled = settled + jnp.dot(
        fitting, arrived.reshape(devices * capacity, 7 * width), precision=lax.Precision.HIGHEST
    )
    final = settled.reshape(blocks, 7, width)
    return (
        final[:, 0:3][None, None],
        final[:, 3:6][None, None],
        final[:, 6][None, None],
        memory[None, None],
    )


def solution(mesh):
    return jax.shard_map(
        local,
        mesh=mesh,
        in_specs=(
            P("axial", "azim", None, None, None),
            P("axial", "azim", None, None, None),
            P("axial", "azim", None, None),
            P("axial", "azim", None, None, None),
            P("axial", "azim", None, None, None, None),
            P("axial", "azim", None, None),
            P("axial", "azim", None),
            P("axial", "azim"),
            P("axial", "azim", None),
        ),
        out_specs=(
            P("axial", "azim", None, None, None),
            P("axial", "azim", None, None, None),
            P("axial", "azim", None, None),
            P("axial", "azim", None, None, None, None),
        ),
        check_vma=False,
    )
```

```python
import functools
import jax
import jax.numpy as jnp
from jax import lax
from jax.experimental import pallas as pl
from jax.experimental.pallas import tpu as pltpu
from jax.sharding import PartitionSpec as P

ITERS = 3
BLK = 32
PAIRS = 64
PB = 128
STEP_TIME = 0.01
GRAVITY_PULL = -9.81
MESH = pl.DeviceIdType.MESH
F32 = jnp.float32
BF16 = jnp.bfloat16


def split3(value):
    hi = value.astype(BF16)
    rest = value - hi.astype(F32)
    mid = rest.astype(BF16)
    lo = (rest - mid.astype(F32)).astype(BF16)
    return hi, mid, lo


def exact_dot(onehot, value):
    out = None
    for part in split3(value):
        term = jnp.dot(onehot, part, preferred_element_type=F32)
        out = term if out is None else out + term
    return out


def near_sums(forces, pairs_f, half, slot):
    for t in range(3):
        pairs_f[t, pl.ds(slot, 1), :] = jnp.sum(jnp.transpose(forces[half, t]), axis=0, keepdims=True)


def contact(codes, ext, near_bc, hist, pairs_f, forces, half, slot):
    code = codes[slot]
    a = code // 256
    c = code % 256
    far = [jnp.broadcast_to(ext[q, pl.ds(c, 1), :], (8, PB)) for q in range(7)]
    column = [None] * 3
    for k in range(16):
        r = slice(8 * k, 8 * k + 8)
        near = [near_bc[a, q, r, :] for q in range(7)]
        d = [near[q] - far[q] for q in range(3)]
        w = [near[q] - far[q] for q in range(3, 6)]
        d2 = jnp.maximum(d[0] * d[0] + d[1] * d[1] + d[2] * d[2], 1e-30)
        rs = lax.rsqrt(d2)
        inv = jnp.minimum(rs, 1.0)
        over = jnp.maximum(near[6] + far[6] - d2 * rs, 0.0)
        root = over * lax.rsqrt(jnp.maximum(over, 1e-30))
        q = (w[0] * d[0] + w[1] * d[1] + w[2] * d[2]) * (inv * inv)
        fade = jnp.minimum(over, 1.0)
        pull = root * (over * inv - 40.0 * q)
        drag = 80.0 * root
        for t in range(3):
            fresh = fade * (hist[slot, t, r, :] + (w[t] - q * d[t]))
            hist[slot, t, r, :] = fresh
            force = pull * d[t] - drag * fresh
            column[t] = force if column[t] is None else column[t] + force
            forces[half, t, r, :] = force
    for t in range(3):
        pairs_f[t, pl.ds(PAIRS + slot, 1), :] = jnp.sum(column[t], axis=0, keepdims=True)


def kernel(sections, sectors, codes, targets, pos, vel, rad, gas, history,
           x_out, v_out, hist,
           ext, near_bc, choose, turned, forces, pairs_f, acting, back, x_own, v_own,
           hist_in_sem, first_send, first_recv, halo_send, halo_recv, back_send, back_recv):
    i = lax.axis_index("axial")
    j = lax.axis_index("azim")
    up = lax.rem(i + 1, sections)
    down = lax.rem(i + sections - 1, sections)
    right = lax.rem(j + 1, sectors)
    left = lax.rem(j + sectors - 1, sectors)
    before = [(down, j), (i, left), (down, left)]
    after = [(up, j), (i, right), (up, right)]

    load = pltpu.make_async_copy(history, hist, hist_in_sem)
    load.start()
    barrier = pltpu.get_barrier_semaphore()
    for peer in before + after:
        pl.semaphore_signal(barrier, inc=1, device_id=peer, device_id_type=MESH)

    for t in range(3):
        x = pos[:, t, :]
        v = vel[:, t, :]
        x_own[t] = x
        v_own[t] = v
        ext[t, 0:BLK, :] = 100.0 * x
        ext[3 + t, 0:BLK, :] = STEP_TIME * v
    ext[6, 0:BLK, :] = 100.0 * rad[...]
    for q in range(7):
        idle = 100.0 if q == 6 else 0.0
        ext[q, 4 * BLK:4 * BLK + 8, :] = jnp.full((8, PB), idle, F32)
        near_bc[BLK, q] = jnp.full((PB, PB), idle, F32)
    row = lax.broadcasted_iota(jnp.int32, (PB, 2 * PB), 0)
    side = lax.broadcasted_iota(jnp.int32, (PB, 2 * PB), 1) // PB

    def make_choice(p, _):
        choose[p] = ((row % BLK == 2 * p + side) & (row < 3 * BLK)).astype(F32).astype(BF16)
        return 0
    lax.fori_loop(0, BLK // 2, make_choice, 0)
    forces[1] = jnp.zeros((3, PB, PB), F32)
    pl.semaphore_wait(barrier, 6)

    def send(planes, sends, recvs):
        copies = []
        for n in range(3):
            copies.append(pltpu.make_async_remote_copy(
                src_ref=ext.at[planes, 0:BLK, :],
                dst_ref=ext.at[planes, (n + 1) * BLK:(n + 2) * BLK, :],
                send_sem=sends.at[n], recv_sem=recvs.at[n],
                device_id=before[n], device_id_type=MESH))
            copies[-1].start()
        return copies

    def turn(planes):
        for n, q in enumerate(planes):
            parts = [part.astype(F32) for part in split3(ext[q, 0:BLK, :])]
            stacked = jnp.concatenate(parts + [jnp.zeros((BLK, PB), F32)], axis=0)
            turned[pl.ds(n * PB, PB), :] = jnp.transpose(stacked).astype(BF16)

    def spread(planes):
        turn(planes)

        def one(p, _):
            wide = jnp.dot(turned[0:len(planes) * PB, :], choose[p], preferred_element_type=F32)
            for n, q in enumerate(planes):
                near_bc[2 * p, q] = wide[n * PB:(n + 1) * PB, :PB]
                near_bc[2 * p + 1, q] = wide[n * PB:(n + 1) * PB, PB:]
            return 0
        lax.fori_loop(0, BLK // 2, one, 0)

    block = lax.broadcasted_iota(jnp.int32, (4 * BLK, PB), 0)
    onehot = (jnp.broadcast_to(targets[...], (4 * BLK, PB)) == block).astype(F32)
    onehot = jnp.where(lax.broadcasted_iota(jnp.int32, (4 * BLK, PB), 1) < PAIRS, onehot, -onehot).astype(BF16)
    mass = rad[...] / 0.06
    mass = mass * mass * mass

    stores = []
    for substep in range(ITERS):
        if substep == 0:
            copies = send(slice(0, 7), first_send, first_recv)
        else:
            copies = send(slice(3, 6), halo_send, halo_recv)
        spread(range(7) if substep == 0 else range(6))
        for copy in copies:
            copy.wait()
        if substep == 0:
            load.wait()
        else:
            for t in range(3):
                ext[t, BLK:4 * BLK, :] = ext[t, BLK:4 * BLK, :] + 100.0 * ext[3 + t, BLK:4 * BLK, :]

        def two_pairs(p, _):
            near_sums(forces, pairs_f, 1, jnp.maximum(2 * p - 1, 0))
            contact(codes, ext, near_bc, hist, pairs_f, forces, 0, 2 * p)
            near_sums(forces, pairs_f, 0, 2 * p)
            contact(codes, ext, near_bc, hist, pairs_f, forces, 1, 2 * p + 1)
            return 0

        lax.fori_loop(0, PAIRS // 2, two_pairs, 0)
        near_sums(forces, pairs_f, 1, PAIRS - 1)

        for t in range(3):
            acting[t] = exact_dot(onehot, pairs_f[t])
        returns = []
        for n in range(3):
            returns.append(pltpu.make_async_remote_copy(
                src_ref=acting.at[:, (n + 1) * BLK:(n + 2) * BLK, :],
                dst_ref=back.at[n],
                send_sem=back_send.at[n], recv_sem=back_recv.at[n],
                device_id=after[n], device_id_type=MESH))
            returns[-1].start()
        for copy in returns:
            copy.wait()
        for t in range(3):
            total = (acting[t, 0:BLK, :] + back[0, t] + back[1, t] + back[2, t]) * 10.0
            v = v_own[t]
            accel = total / mass + (gas[:, t, :] - v) / 0.05
            if t == 1:
                accel = accel + GRAVITY_PULL
            v = v + STEP_TIME * accel
            x = x_own[t] + STEP_TIME * v
            v_own[t] = v
            x_own[t] = x
            ext[t, 0:BLK, :] = 100.0 * x
            ext[3 + t, 0:BLK, :] = STEP_TIME * v
    x_out[...] = x_own[...]
    v_out[...] = v_own[...]


def substeps(sections, sectors, codes, targets, pos, vel, rad, gas, history):
    vmem = pl.BlockSpec(memory_space=pltpu.VMEM)
    plane = jax.ShapeDtypeStruct((3, BLK, PB), F32)
    return pl.pallas_call(
        functools.partial(kernel, sections, sectors),
        out_shape=(plane, plane, pltpu.VMEM(history.shape, F32)),
        in_specs=[pl.BlockSpec(memory_space=pltpu.SMEM)] + [vmem] * 5 + [pl.BlockSpec(memory_space=pl.ANY)],
        out_specs=(vmem, vmem, vmem),
        scratch_shapes=[
            pltpu.VMEM((7, 4 * BLK + 8, PB), F32),
            pltpu.VMEM((BLK + 1, 7, PB, PB), F32),
            pltpu.VMEM((BLK // 2, PB, 2 * PB), BF16),
            pltpu.VMEM((7 * PB, PB), BF16),
            pltpu.VMEM((2, 3, PB, PB), F32),
            pltpu.VMEM((3, 2 * PAIRS, PB), F32),
            pltpu.VMEM((3, 4 * BLK, PB), F32),
            pltpu.VMEM((3, 3, BLK, PB), F32),
            pltpu.VMEM((3, BLK, PB), F32),
            pltpu.VMEM((3, BLK, PB), F32),
            pltpu.SemaphoreType.DMA,
            pltpu.SemaphoreType.DMA((3,)),
            pltpu.SemaphoreType.DMA((3,)),
            pltpu.SemaphoreType.DMA((3,)),
            pltpu.SemaphoreType.DMA((3,)),
            pltpu.SemaphoreType.DMA((3,)),
            pltpu.SemaphoreType.DMA((3,)),
        ],
        compiler_params=pltpu.CompilerParams(collective_id=0, has_side_effects=True, vmem_limit_bytes=32 << 20),
        name="substeps",
    )(codes, targets, pos, vel, rad, gas, history)


CAP = 3
LANES = 128


def repeated(value):
    return jnp.transpose(value)


def count_before(same, width):
    rows, cols = same.shape
    earlier = lax.broadcasted_iota(jnp.int32, same.shape, 1) < lax.broadcasted_iota(jnp.int32, same.shape, 0)
    marked = (same & earlier).astype(F32).astype(BF16)
    return jnp.dot(marked, jnp.ones((cols, width), BF16), preferred_element_type=F32)


def resettle(sections, sectors, x, v, rad, home, x_out, v_out, r_out,
             outgoing, gathered, handed, arrived,
             a_send, a_recv, b_send, b_recv, c_send, c_recv):
    i = lax.axis_index("axial")
    j = lax.axis_index("azim")
    ranks = BLK // 4
    part = ranks * CAP
    k = lax.rem(j, ranks)
    base = j - k
    a_peers = [lax.rem(k + o, ranks) for o in range(1, ranks)]
    b_peers = [lax.rem(i + o, sections) for o in range(1, sections)]
    c_peers = [lax.rem(j + o, sectors) for o in range(1, sectors)]
    barrier = pltpu.get_barrier_semaphore()
    for peer in b_peers:
        pl.semaphore_signal(barrier, inc=1, device_id=(peer, j), device_id_type=MESH)
    for peer in c_peers:
        pl.semaphore_signal(barrier, inc=1, device_id=(i, peer), device_id_type=MESH)
    myself = (i * sectors + j).astype(F32)

    label = jnp.broadcast_to(home[...], (LANES, LANES))
    target = jnp.floor((label - 1.0) * (1.0 / BLK))
    target_col = repeated(target)
    real = lax.broadcasted_iota(jnp.int32, (LANES, LANES), 1) < BLK
    rank_col = count_before((target_col == target) & real, LANES)
    rank = repeated(rank_col)
    place_col = count_before((rank_col == rank) & (target != myself) & real, LANES)
    row = jnp.where((target != myself) & real, rank * CAP + repeated(place_col), -1.0)
    order = lax.broadcasted_iota(jnp.int32, (part, LANES), 0).astype(F32)
    pick = (row[0:part, :] == order).astype(F32).astype(BF16)
    label_col = repeated(label)

    own = [x[t] for t in range(3)] + [v[t] for t in range(3)] + [rad[...], label_col[0:BLK, :]]
    wide = jnp.concatenate(own, axis=1)
    packed = exact_dot(pick[:, 0:BLK], wide)
    for t in range(8):
        outgoing[:, t, :] = packed[:, t * PB:(t + 1) * PB]
    gathered[sections * part:, :, :] = jnp.zeros((gathered.shape[0] - sections * part, 8, PB), F32)
    pl.semaphore_wait(barrier, sections + sectors - 2)

    copies = []
    for o, peer in enumerate(a_peers):
        copies.append(pltpu.make_async_remote_copy(
            src_ref=outgoing.at[pl.ds(peer * CAP, CAP)],
            dst_ref=gathered.at[pl.ds(i * part + k * CAP, CAP)],
            send_sem=a_send.at[o], recv_sem=a_recv.at[o],
            device_id=(i, base + peer), device_id_type=MESH))
        copies[-1].start()
    gathered[pl.ds(i * part + k * CAP, CAP)] = outgoing[pl.ds(k * CAP, CAP)]
    for copy in copies:
        copy.wait()

    copies = []
    for o, peer in enumerate(b_peers):
        copies.append(pltpu.make_async_remote_copy(
            src_ref=gathered.at[pl.ds(i * part, part)],
            dst_ref=gathered.at[pl.ds(i * part, part)],
            send_sem=b_send.at[o], recv_sem=b_recv.at[o],
            device_id=(peer, j), device_id_type=MESH))
        copies[-1].start()
    for copy in copies:
        copy.wait()

    held = sections * part
    total = gathered.shape[0]
    label_col = gathered[:, 7, :]
    target_col = jnp.floor((label_col - 1.0) * (1.0 / BLK))
    target = repeated(target_col)
    target_row = jnp.concatenate([target] * (total // LANES), axis=0)
    target_wide = jnp.concatenate([target_col] * (total // LANES), axis=1)
    q_col = count_before(target_wide == target_row, LANES)
    toward = target_col - (i * sectors).astype(F32)
    here = (toward >= 0.0) & (toward < float(sectors)) & (label_col > 0.0)
    key = repeated(jnp.where(here, toward * CAP + q_col, -1.0))
    order = lax.broadcasted_iota(jnp.int32, (sectors * CAP, total), 0).astype(F32)
    pick = (key[0:sectors * CAP, :] == order).astype(F32).astype(BF16)
    wide = jnp.concatenate([gathered[:, t, :] for t in range(8)], axis=1)
    packed = exact_dot(pick, wide)
    for t in range(8):
        handed[:, t, :] = packed[:, t * PB:(t + 1) * PB]

    copies = []
    for o, peer in enumerate(c_peers):
        copies.append(pltpu.make_async_remote_copy(
            src_ref=handed.at[pl.ds(peer * CAP, CAP)],
            dst_ref=arrived.at[pl.ds(j * CAP, CAP)],
            send_sem=c_send.at[o], recv_sem=c_recv.at[o],
            device_id=(i, peer), device_id_type=MESH))
        copies[-1].start()
    arrived[pl.ds(j * CAP, CAP)] = handed[pl.ds(j * CAP, CAP)]
    for copy in copies:
        copy.wait()

    count = sectors * CAP
    rest = jnp.zeros((LANES - BLK - count, PB), F32)
    both = [jnp.concatenate([own[t], arrived[:, t, :], rest], axis=0) for t in range(8)]
    slot = repeated(both[7] - 1.0 - myself * BLK)
    order = lax.broadcasted_iota(jnp.int32, (BLK, LANES), 0).astype(F32)
    pick = (slot[0:BLK, :] == order).astype(F32).astype(BF16)
    settled = exact_dot(pick, jnp.concatenate(both[0:7], axis=1))
    for t in range(3):
        x_out[t] = settled[:, t * PB:(t + 1) * PB]
        v_out[t] = settled[:, (3 + t) * PB:(4 + t) * PB]
    r_out[...] = settled[:, 6 * PB:7 * PB]


def rebalance(sections, sectors, x, v, rad, home):
    vmem = pl.BlockSpec(memory_space=pltpu.VMEM)
    part = BLK // 4 * CAP
    total = -(-sections * part // LANES) * LANES
    plane = jax.ShapeDtypeStruct((3, BLK, PB), F32)
    sems = [pltpu.SemaphoreType.DMA((n,)) for n in (BLK // 4 - 1, sections - 1, sectors - 1) for _ in range(2)]
    return pl.pallas_call(
        functools.partial(resettle, sections, sectors),
        out_shape=(plane, plane, jax.ShapeDtypeStruct((BLK, PB), F32)),
        in_specs=[vmem] * 4,
        out_specs=(vmem, vmem, vmem),
        scratch_shapes=[
            pltpu.VMEM((part, 8, PB), F32),
            pltpu.VMEM((total, 8, PB), F32),
            pltpu.VMEM((sectors * CAP, 8, PB), F32),
            pltpu.VMEM((sectors * CAP, 8, PB), F32),
        ] + sems,
        compiler_params=pltpu.CompilerParams(collective_id=1, has_side_effects=True, vmem_limit_bytes=16 << 20),
        name="rebalance",
    )(x, v, rad, home)


def local(
    positions,
    velocities,
    radius,
    gas_velocity,
    history,
    pair_list,
    history_slot,
    pair_count,
    new_home,
):
    radii = radius[0, 0]
    order = jnp.arange(PAIRS, dtype=jnp.int32)
    chosen = (history_slot[0, 0][None, :] == order[:, None]) & (order < pair_count[0, 0])[None, :]
    idle = BLK * 256 + 4 * BLK
    code = pair_list[0, 0, 0] * 256 + pair_list[0, 0, 1] - idle
    codes = idle + jnp.sum(jnp.where(chosen, code[None, :], 0), axis=1)
    near = jnp.where(codes == idle, 4 * BLK, codes // 256)
    targets = jnp.concatenate([near, codes % 256])[None, :]
    sections = lax.axis_size("axial")
    sectors = lax.axis_size("azim")
    place, speed, memory = substeps(
        sections, sectors, codes, targets,
        positions[0, 0], velocities[0, 0], radii, gas_velocity[0, 0], history[0, 0])
    home = jnp.concatenate([(new_home[0, 0] + 1).astype(F32), jnp.zeros((LANES - BLK,), F32)])[None, :]
    place, speed, radii = rebalance(sections, sectors, place, speed, radii, home)
    return (
        jnp.transpose(place, (1, 0, 2))[None, None],
        jnp.transpose(speed, (1, 0, 2))[None, None],
        radii[None, None],
        memory[None, None],
    )


def solution(mesh):
    return jax.shard_map(
        local,
        mesh=mesh,
        in_specs=(
            P("axial", "azim", None, None, None),
            P("axial", "azim", None, None, None),
            P("axial", "azim", None, None),
            P("axial", "azim", None, None, None),
            P("axial", "azim", None, None, None, None),
            P("axial", "azim", None, None),
            P("axial", "azim", None),
            P("axial", "azim"),
            P("axial", "azim", None),
        ),
        out_specs=(
            P("axial", "azim", None, None, None),
            P("axial", "azim", None, None, None),
            P("axial", "azim", None, None),
            P("axial", "azim", None, None, None, None),
        ),
        check_vma=False,
    )
```

```python
import functools
import jax
import jax.numpy as jnp
from jax import lax
from jax.experimental import pallas as pl
from jax.experimental.pallas import tpu as pltpu
from jax.sharding import PartitionSpec as P

ITERS = 3
BLK = 32
PAIRS = 64
PB = 128
CAP = 3
FIRST_PART = 20
STEP_TIME = 0.01
GRAVITY_PULL = -9.81
MESH = pl.DeviceIdType.MESH
F32 = jnp.float32
BF16 = jnp.bfloat16


def split3(value):
    hi = value.astype(BF16)
    rest = value - hi.astype(F32)
    mid = rest.astype(BF16)
    lo = (rest - mid.astype(F32)).astype(BF16)
    return hi, mid, lo


def exact_dot(onehot, value):
    out = None
    for part in split3(value):
        term = jnp.dot(onehot, part, preferred_element_type=F32)
        out = term if out is None else out + term
    return out


def near_sums(forces, pairs_f, half, slot):
    for t in range(3):
        pairs_f[t, pl.ds(slot, 1), :] = jnp.sum(jnp.transpose(forces[half, t]), axis=0, keepdims=True)


def contact(codes, ext, near_bc, hist, pairs_f, forces, half, slot):
    code = codes[0, slot]
    a = code // 256
    c = code % 256
    far = [jnp.broadcast_to(ext[q, pl.ds(c, 1), :], (8, PB)) for q in range(7)]
    column = [None] * 3
    for k in range(16):
        r = slice(8 * k, 8 * k + 8)
        near = [near_bc[a, q, r, :] for q in range(7)]
        d = [near[q] - far[q] for q in range(3)]
        w = [near[q] - far[q] for q in range(3, 6)]
        d2 = jnp.maximum(d[0] * d[0] + d[1] * d[1] + d[2] * d[2], 1e-30)
        rs = lax.rsqrt(d2)
        inv = jnp.minimum(rs, 1.0)
        over = jnp.maximum(near[6] + far[6] - d2 * rs, 0.0)
        root = over * lax.rsqrt(jnp.maximum(over, 1e-30))
        q = (w[0] * d[0] + w[1] * d[1] + w[2] * d[2]) * (inv * inv)
        fade = jnp.minimum(over, 1.0)
        pull = root * (over * inv - 40.0 * q)
        drag = 80.0 * root
        for t in range(3):
            fresh = fade * (hist[slot, t, r, :] + (w[t] - q * d[t]))
            hist[slot, t, r, :] = fresh
            force = pull * d[t] - drag * fresh
            column[t] = force if column[t] is None else column[t] + force
            forces[half, t, r, :] = force
    for t in range(3):
        pairs_f[t, pl.ds(PAIRS + slot, 1), :] = jnp.sum(column[t], axis=0, keepdims=True)


def count_before(same):
    earlier = lax.broadcasted_iota(jnp.int32, same.shape, 1) < lax.broadcasted_iota(jnp.int32, same.shape, 0)
    marked = (same & earlier).astype(F32).astype(BF16)
    return jnp.dot(marked, jnp.ones((same.shape[1], PB), BF16), preferred_element_type=F32)


def chosen_rows(row_of, count):
    order = lax.broadcasted_iota(jnp.int32, (count, row_of.shape[1]), 0).astype(F32)
    return (row_of[0:count, :] == order).astype(F32).astype(BF16)


def kernel(sections, sectors, pairs_in, slots_in, home_in, pos, vel, rad, gas, history, count,
           x_out, v_out, r_out, hist,
           x_own, v_own, r_own, g_own, pairs, slots, home, tables, columns, codes,
           ext, near_bc, choose, turned, forces, pairs_f, acting, back,
           pick_a, pick_c, pick_f,
           out_x, all_x, hand_x, come_x, out_v, all_v, hand_v, come_v,
           load_sem, first_send, first_recv, halo_send, halo_recv, back_send, back_recv,
           a_send, a_recv, b_send, b_recv, c_send, c_recv):
    i = lax.axis_index("axial")
    j = lax.axis_index("azim")
    up = lax.rem(i + 1, sections)
    down = lax.rem(i + sections - 1, sections)
    right = lax.rem(j + 1, sectors)
    left = lax.rem(j + sectors - 1, sectors)
    before = [(down, j), (i, left), (down, left)]
    after = [(up, j), (i, right), (up, right)]
    ranks = BLK // 4
    part = ranks * CAP
    k = lax.rem(j, ranks)
    a_peers = [lax.rem(k + o, ranks) for o in range(1, ranks)]
    b_peers = [lax.rem(i + o, sections) for o in range(1, sections)]
    c_peers = [lax.rem(j + o, sectors) for o in range(1, sectors)]
    myself = (i * sectors + j).astype(F32)

    loads = [pltpu.make_async_copy(src, dst, load_sem.at[n]) for n, (src, dst) in enumerate(
        [(pos, x_own), (vel, v_own), (rad, r_own), (pairs_in, pairs), (slots_in, slots),
         (home_in, home), (gas, g_own), (history, hist)])]
    for load in loads:
        load.start()
    barrier = pltpu.get_barrier_semaphore()
    peers = [(peer, j) for peer in b_peers] + [(i, peer) for peer in c_peers] + [before[2], after[2]]
    for peer in peers:
        pl.semaphore_signal(barrier, inc=1, device_id=peer, device_id_type=MESH)

    for load in loads[0:6]:
        load.wait()
    for t in range(3):
        ext[t, 0:BLK, :] = 100.0 * x_own[t]
        ext[3 + t, 0:BLK, :] = STEP_TIME * v_own[t]
    ext[6, 0:BLK, :] = 100.0 * r_own[...]
    for q in range(7):
        idle = 100.0 if q == 6 else 0.0
        ext[q, 4 * BLK:4 * BLK + 8, :] = jnp.full((8, PB), idle, F32)
        near_bc[BLK, q] = jnp.full((PB, PB), idle, F32)
    row = lax.broadcasted_iota(jnp.int32, (PB, 2 * PB), 0)
    side = lax.broadcasted_iota(jnp.int32, (PB, 2 * PB), 1) // PB

    def make_choice(p, _):
        choose[p] = ((row % BLK == 2 * p + side) & (row < 3 * BLK)).astype(F32).astype(BF16)
        return 0
    lax.fori_loop(0, BLK // 2, make_choice, 0)
    forces[1] = jnp.zeros((3, PB, PB), F32)

    tables[...] = jnp.zeros(tables.shape, jnp.int32)
    tables[0:2, 0:PAIRS] = pairs[...]
    tables[2:3, 0:PAIRS] = slots[...]
    place = lax.broadcasted_iota(jnp.int32, (PB, PB), 0)
    idle = BLK * 256 + 4 * BLK
    code = jnp.transpose(jnp.broadcast_to(tables[0:1, :] * 256 + tables[1:2, :] - idle, (PB, PB)))
    slot = jnp.transpose(jnp.broadcast_to(tables[2:3, :], (PB, PB)))
    active = (place < count[0, 0]) & (place < PAIRS)
    here = (slot == lax.broadcasted_iota(jnp.int32, (PB, PB), 1) % PAIRS) & active
    columns[...] = jnp.broadcast_to(idle + jnp.sum(jnp.where(here, code, 0), axis=0, keepdims=True), columns.shape)
    fetch = pltpu.make_async_copy(columns, codes, load_sem.at[8])
    fetch.start()
    pl.semaphore_wait(barrier, len(peers))

    def send(planes, sends, recvs):
        copies = []
        for n in range(3):
            copies.append(pltpu.make_async_remote_copy(
                src_ref=ext.at[planes, 0:BLK, :],
                dst_ref=ext.at[planes, (n + 1) * BLK:(n + 2) * BLK, :],
                send_sem=sends.at[n], recv_sem=recvs.at[n],
                device_id=before[n], device_id_type=MESH))
            copies[-1].start()
        return copies

    def spread(planes):
        for n, q in enumerate(planes):
            parts = [piece.astype(F32) for piece in split3(ext[q, 0:BLK, :])]
            stacked = jnp.concatenate(parts + [jnp.zeros((BLK, PB), F32)], axis=0)
            turned[pl.ds(n * PB, PB), :] = jnp.transpose(stacked).astype(BF16)

        def one(p, _):
            wide = jnp.dot(turned[0:len(planes) * PB, :], choose[p], preferred_element_type=F32)
            for n, q in enumerate(planes):
                near_bc[2 * p, q] = wide[n * PB:(n + 1) * PB, :PB]
                near_bc[2 * p + 1, q] = wide[n * PB:(n + 1) * PB, PB:]
            return 0
        lax.fori_loop(0, BLK // 2, one, 0)

    def two_pairs(p, _):
        near_sums(forces, pairs_f, 1, jnp.maximum(2 * p - 1, 0))
        contact(codes, ext, near_bc, hist, pairs_f, forces, 0, 2 * p)
        near_sums(forces, pairs_f, 0, 2 * p)
        contact(codes, ext, near_bc, hist, pairs_f, forces, 1, 2 * p + 1)
        return 0

    def sort_own():
        tables[3:4, 0:BLK] = home[...] + 1
        label = jnp.broadcast_to(tables[3:4, :].astype(F32), (PB, PB))
        target = jnp.floor((label - 1.0) * (1.0 / BLK))
        real = lax.broadcasted_iota(jnp.int32, (PB, PB), 1) < BLK
        rank_col = count_before((jnp.transpose(target) == target) & real)
        rank = jnp.transpose(rank_col)
        place_col = count_before((rank_col == rank) & (target != myself) & real)
        place = jnp.where((target != myself) & real, rank * CAP + jnp.transpose(place_col), -1.0)
        pick_a[...] = chosen_rows(place, BLK)
        return jnp.transpose(label)[0:BLK, :]

    def pack(pick, blocks_in, out):
        packed = exact_dot(pick, jnp.concatenate(blocks_in, axis=1))
        for t in range(len(blocks_in)):
            out[:, t, :] = packed[0:out.shape[0], t * PB:(t + 1) * PB]

    def hop_a(which, out, everything):
        copies = []
        for o, peer in enumerate(a_peers):
            copies.append(pltpu.make_async_remote_copy(
                src_ref=out.at[pl.ds(peer * CAP, CAP)],
                dst_ref=everything.at[pl.ds(i * part + k * CAP, CAP)],
                send_sem=a_send.at[which, o], recv_sem=a_recv.at[which, o],
                device_id=(i, j - k + peer), device_id_type=MESH))
            copies[-1].start()
        everything[pl.ds(i * part + k * CAP, CAP)] = out[pl.ds(k * CAP, CAP)]
        return copies

    def hop_b(which, everything):
        copies = []
        for o, peer in enumerate(b_peers):
            copies.append(pltpu.make_async_remote_copy(
                src_ref=everything.at[pl.ds(i * part, part)],
                dst_ref=everything.at[pl.ds(i * part, part)],
                send_sem=b_send.at[which, o], recv_sem=b_recv.at[which, o],
                device_id=(peer, j), device_id_type=MESH))
            copies[-1].start()
        return copies

    def sort_all():
        total = all_x.shape[0]
        label_col = all_x[:, 4, :]
        target_col = jnp.floor((label_col - 1.0) * (1.0 / BLK))
        target_row = jnp.concatenate([jnp.transpose(target_col)] * (total // PB), axis=0)
        target_wide = jnp.concatenate([target_col] * (total // PB), axis=1)
        place_col = count_before(target_wide == target_row)
        toward = target_col - (i * sectors).astype(F32)
        here = (toward >= 0.0) & (toward < float(sectors)) & (label_col > 0.0)
        pick_c[...] = chosen_rows(jnp.transpose(jnp.where(here, toward * CAP + place_col, -1.0)), sectors * CAP)

    def hop_c(which, out, come):
        copies = []
        for o, peer in enumerate(c_peers):
            copies.append(pltpu.make_async_remote_copy(
                src_ref=out.at[pl.ds(peer * CAP, CAP)],
                dst_ref=come.at[pl.ds(j * CAP, CAP)],
                send_sem=c_send.at[which, o], recv_sem=c_recv.at[which, o],
                device_id=(i, peer), device_id_type=MESH))
            copies[-1].start()
        come[pl.ds(j * CAP, CAP)] = out[pl.ds(j * CAP, CAP)]
        return copies

    def wait(copies):
        for copy in copies:
            copy.wait()

    def candidates(own, come):
        rest = jnp.zeros((PB - BLK - sectors * CAP, PB), F32)
        return [jnp.concatenate([mine, come[:, t, :], rest], axis=0) for t, mine in enumerate(own)]

    block = lax.broadcasted_iota(jnp.int32, (4 * BLK, PB), 0)
    lane = lax.broadcasted_iota(jnp.int32, (4 * BLK, PB), 1)
    code = jnp.broadcast_to(columns[0:1, :], (4 * BLK, PB))
    near = code // 256
    near = jnp.where(near < BLK, near, 4 * BLK)
    onehot = (jnp.where(lane < PAIRS, near, code % 256) == block).astype(F32)
    onehot = jnp.where(lane < PAIRS, onehot, -onehot).astype(BF16)
    mass = r_own[...] / 0.06
    mass = mass * mass * mass

    for substep in range(ITERS):
        last = substep == ITERS - 1
        if substep == 0:
            copies = send(slice(0, 7), first_send, first_recv)
        else:
            copies = send(slice(3, 6), halo_send, halo_recv)
        if last:
            early = [x_own[t] for t in range(3)] + [r_own[...], own_label]
            pack(pick_a[:, 0:BLK], early, out_x)
            first_hop = hop_a(0, out_x, all_x)
        spread(range(7) if substep == 0 else range(6))
        if substep == 0:
            own_label = sort_own()
            out_x[:, 5:8, :] = jnp.zeros((part, 3, PB), F32)
            hand_x[:, 5:8, :] = jnp.zeros((sectors * CAP, 3, PB), F32)
            out_v[...] = jnp.zeros(out_v.shape, F32)
            hand_v[...] = jnp.zeros(hand_v.shape, F32)
            held = sections * part
            all_x[held:] = jnp.zeros((all_x.shape[0] - held,) + all_x.shape[1:], F32)
            all_v[held:] = jnp.zeros((all_v.shape[0] - held,) + all_v.shape[1:], F32)
        wait(copies)
        if substep == 0:
            wait(loads[6:])
            fetch.wait()
        else:
            for t in range(3):
                ext[t, BLK:4 * BLK, :] = ext[t, BLK:4 * BLK, :] + 100.0 * ext[3 + t, BLK:4 * BLK, :]

        if last:
            wait(first_hop)
            second_hop = hop_b(0, all_x)
            lax.fori_loop(0, FIRST_PART, two_pairs, 0)
            wait(second_hop)
            sort_all()
            pack(pick_c[...], [all_x[:, t, :] for t in range(5)], hand_x)
            third_hop = hop_c(0, hand_x, come_x)
            lax.fori_loop(FIRST_PART, PAIRS // 2, two_pairs, 0)
        else:
            lax.fori_loop(0, PAIRS // 2, two_pairs, 0)
        near_sums(forces, pairs_f, 1, PAIRS - 1)

        for t in range(3):
            acting[t] = exact_dot(onehot, pairs_f[t])
        returns = []
        for n in range(3):
            returns.append(pltpu.make_async_remote_copy(
                src_ref=acting.at[:, (n + 1) * BLK:(n + 2) * BLK, :],
                dst_ref=back.at[n],
                send_sem=back_send.at[n], recv_sem=back_recv.at[n],
                device_id=after[n], device_id_type=MESH))
            returns[-1].start()
        if last:
            wait(third_hop)
            both = candidates(early, come_x)
            pick_f[...] = chosen_rows(jnp.transpose(both[4] - 1.0 - myself * BLK), BLK)
            settled = exact_dot(pick_f[...], jnp.concatenate(both[0:4], axis=1))
            for t in range(3):
                x_out[t] = settled[:, t * PB:(t + 1) * PB]
            r_out[...] = settled[:, 3 * PB:4 * PB]
        wait(returns)
        for t in range(3):
            total = (acting[t, 0:BLK, :] + back[0, t] + back[1, t] + back[2, t]) * 10.0
            v = v_own[t]
            accel = total / mass + (g_own[t] - v) / 0.05
            if t == 1:
                accel = accel + GRAVITY_PULL
            v = v + STEP_TIME * accel
            v_own[t] = v
            if not last:
                x = x_own[t] + STEP_TIME * v
                x_own[t] = x
                ext[t, 0:BLK, :] = 100.0 * x
                ext[3 + t, 0:BLK, :] = STEP_TIME * v

    own = [v_own[t] for t in range(3)]
    pack(pick_a[:, 0:BLK], own, out_v)
    wait(hop_a(1, out_v, all_v))
    wait(hop_b(1, all_v))
    pack(pick_c[...], [all_v[:, t, :] for t in range(3)], hand_v)
    wait(hop_c(1, hand_v, come_v))
    settled = exact_dot(pick_f[...], jnp.concatenate(candidates(own, come_v), axis=1))
    for t in range(3):
        v = settled[:, t * PB:(t + 1) * PB]
        v_out[t] = v
        x_out[t] = x_out[t] + STEP_TIME * v


def substeps(sections, sectors, pairs, slots, count, home, pos, vel, rad, gas, history):
    vmem = pl.BlockSpec(memory_space=pltpu.VMEM)
    hbm = pl.BlockSpec(memory_space=pltpu.HBM)
    plane = jax.ShapeDtypeStruct((3, BLK, PB), F32)
    part = BLK // 4 * CAP
    total = -(-sections * part // PB) * PB
    three = pltpu.SemaphoreType.DMA((3,))
    hops = [pltpu.SemaphoreType.DMA((2, n)) for n in (BLK // 4 - 1, sections - 1, sectors - 1) for _ in range(2)]
    return pl.pallas_call(
        functools.partial(kernel, sections, sectors),
        out_shape=(plane, plane, jax.ShapeDtypeStruct((BLK, PB), F32), pltpu.VMEM(history.shape, F32)),
        in_specs=[hbm] * 8 + [pl.BlockSpec(memory_space=pltpu.SMEM)],
        out_specs=(vmem, vmem, vmem, vmem),
        scratch_shapes=[
            pltpu.VMEM((3, BLK, PB), F32),
            pltpu.VMEM((3, BLK, PB), F32),
            pltpu.VMEM((BLK, PB), F32),
            pltpu.VMEM((3, BLK, PB), F32),
            pltpu.VMEM(pairs.shape, jnp.int32),
            pltpu.VMEM(slots.shape, jnp.int32),
            pltpu.VMEM(home.shape, jnp.int32),
            pltpu.VMEM((8, PB), jnp.int32),
            pltpu.VMEM((8, PB), jnp.int32),
            pltpu.SMEM((8, PB), jnp.int32),
            pltpu.VMEM((7, 4 * BLK + 8, PB), F32),
            pltpu.VMEM((BLK + 1, 7, PB, PB), F32),
            pltpu.VMEM((BLK // 2, PB, 2 * PB), BF16),
            pltpu.VMEM((7 * PB, PB), BF16),
            pltpu.VMEM((2, 3, PB, PB), F32),
            pltpu.VMEM((3, 2 * PAIRS, PB), F32),
            pltpu.VMEM((3, 4 * BLK, PB), F32),
            pltpu.VMEM((3, 3, BLK, PB), F32),
            pltpu.VMEM((BLK, PB), BF16),
            pltpu.VMEM((sectors * CAP, total), BF16),
            pltpu.VMEM((BLK, PB), BF16),
        ] + [
            pltpu.VMEM((count, rows, PB), F32)
            for rows in (8, 4) for count in (part, total, sectors * CAP, sectors * CAP)
        ] + [pltpu.SemaphoreType.DMA((9,))] + [three] * 6 + hops,
        compiler_params=pltpu.CompilerParams(collective_id=0, has_side_effects=True, vmem_limit_bytes=32 << 20),
        name="substeps",
    )(*[pltpu.with_memory_space_constraint(a, pltpu.HBM)
        for a in (pairs, slots, home, pos, vel, rad, gas, history)], count)


def hand_over(x, v, r, hist, x_out, v_out, r_out, hist_out, sems):
    copies = [pltpu.make_async_copy(x, x_out, sems.at[0]),
              pltpu.make_async_copy(v, v_out, sems.at[1]),
              pltpu.make_async_copy(r, r_out, sems.at[2])]
    group = PAIRS // 8
    for n in range(8):
        rows = pl.ds(n * group, group)
        copies.append(pltpu.make_async_copy(hist.at[rows], hist_out.at[rows], sems.at[3 + n]))
    for copy in copies:
        copy.start()
    for copy in copies:
        copy.wait()


def results(x, v, r, hist):
    vmem = pl.BlockSpec(memory_space=pltpu.VMEM)
    hbm = pl.BlockSpec(memory_space=pl.ANY)
    return pl.pallas_call(
        hand_over,
        out_shape=tuple(jax.ShapeDtypeStruct(a.shape, F32) for a in (x, v, r, hist)),
        in_specs=[vmem] * 4,
        out_specs=(hbm,) * 4,
        scratch_shapes=[pltpu.SemaphoreType.DMA((11,))],
        compiler_params=pltpu.CompilerParams(vmem_limit_bytes=16 << 20),
        name="results",
    )(x, v, r, hist)


def local(
    positions,
    velocities,
    radius,
    gas_velocity,
    history,
    pair_list,
    history_slot,
    pair_count,
    new_home,
):
    def planes(array):
        return jnp.transpose(array[0, 0], (1, 0, 2))

    place, speed, radii, memory = results(*substeps(
        lax.axis_size("axial"), lax.axis_size("azim"), pair_list[0, 0], history_slot[0], pair_count, new_home[0],
        planes(positions), planes(velocities), radius[0, 0], planes(gas_velocity), history[0, 0]))
    return (
        jnp.transpose(place, (1, 0, 2))[None, None],
        jnp.transpose(speed, (1, 0, 2))[None, None],
        radii[None, None],
        memory[None, None],
    )


def solution(mesh):
    return jax.shard_map(
        local,
        mesh=mesh,
        in_specs=(
            P("axial", "azim", None, None, None),
            P("axial", "azim", None, None, None),
            P("axial", "azim", None, None),
            P("axial", "azim", None, None, None),
            P("axial", "azim", None, None, None, None),
            P("axial", "azim", None, None),
            P("axial", "azim", None),
            P("axial", "azim"),
            P("axial", "azim", None),
        ),
        out_specs=(
            P("axial", "azim", None, None, None),
            P("axial", "azim", None, None, None),
            P("axial", "azim", None, None),
            P("axial", "azim", None, None, None, None),
        ),
        check_vma=False,
    )
```

```python
import functools
import jax
import jax.numpy as jnp
from jax import lax
from jax.experimental import pallas as pl
from jax.experimental.pallas import tpu as pltpu
from jax.sharding import PartitionSpec as P

ITERS = 3
BLK = 32
PAIRS = 64
PB = 128
CAP = 3
FIRST_PART = 24
STEP_TIME = 0.01
GRAVITY_PULL = -9.81
MESH = pl.DeviceIdType.MESH
F32 = jnp.float32
BF16 = jnp.bfloat16


def split3(value):
    hi = value.astype(BF16)
    rest = value - hi.astype(F32)
    mid = rest.astype(BF16)
    lo = (rest - mid.astype(F32)).astype(BF16)
    return hi, mid, lo


def exact_dot(onehot, value):
    out = None
    for part in split3(value):
        term = jnp.dot(onehot, part, preferred_element_type=F32)
        out = term if out is None else out + term
    return out


def near_sums(forces, pairs_f, half, slot):
    for t in range(3):
        pairs_f[t, pl.ds(slot, 1), :] = jnp.sum(jnp.transpose(forces[half, t]), axis=0, keepdims=True)


def contact(codes, ext, near_bc, hist, pairs_f, forces, half, slot):
    code = codes[0, slot]
    a = code // 256
    c = code % 256
    far = [jnp.broadcast_to(ext[q, pl.ds(c, 1), :], (8, PB)) for q in range(7)]
    column = [None] * 3
    for k in range(16):
        r = slice(8 * k, 8 * k + 8)
        near = [near_bc[a, q, r, :] for q in range(7)]
        d = [near[q] - far[q] for q in range(3)]
        w = [near[q] - far[q] for q in range(3, 6)]
        d2 = jnp.maximum(d[0] * d[0] + d[1] * d[1] + d[2] * d[2], 1e-30)
        rs = lax.rsqrt(d2)
        inv = jnp.minimum(rs, 1.0)
        over = jnp.maximum(near[6] + far[6] - d2 * rs, 0.0)
        root = over * lax.rsqrt(jnp.maximum(over, 1e-30))
        q = (w[0] * d[0] + w[1] * d[1] + w[2] * d[2]) * (inv * inv)
        fade = jnp.minimum(over, 1.0)
        pull = root * (over * inv - 40.0 * q)
        drag = 80.0 * root
        for t in range(3):
            fresh = fade * (hist[slot, t, r, :] + (w[t] - q * d[t]))
            hist[slot, t, r, :] = fresh
            force = pull * d[t] - drag * fresh
            column[t] = force if column[t] is None else column[t] + force
            forces[half, t, r, :] = force
    for t in range(3):
        pairs_f[t, pl.ds(PAIRS + slot, 1), :] = jnp.sum(column[t], axis=0, keepdims=True)


def count_before(same):
    earlier = lax.broadcasted_iota(jnp.int32, same.shape, 1) < lax.broadcasted_iota(jnp.int32, same.shape, 0)
    marked = (same & earlier).astype(F32).astype(BF16)
    return jnp.dot(marked, jnp.ones((same.shape[1], PB), BF16), preferred_element_type=F32)


def chosen_rows(row_of, count):
    order = lax.broadcasted_iota(jnp.int32, (count, row_of.shape[1]), 0).astype(F32)
    return (row_of[0:count, :] == order).astype(F32).astype(BF16)


def kernel(sections, sectors, pairs_in, slots_in, home_in, pos, vel, rad, gas, history, count,
           x_out, v_out, r_out, hist,
           x_own, v_own, r_own, g_own, pairs, slots, home, tables, columns, codes,
           ext, near_bc, choose, turned, forces, pairs_f, acting, back,
           pick_a, pick_c, pick_f,
           out_x, all_x, hand_x, come_x, out_v, all_v, hand_v, come_v,
           load_sem, first_send, first_recv, halo_send, halo_recv, back_send, back_recv,
           a_send, a_recv, b_send, b_recv, c_send, c_recv):
    i = lax.axis_index("axial")
    j = lax.axis_index("azim")
    up = lax.rem(i + 1, sections)
    down = lax.rem(i + sections - 1, sections)
    right = lax.rem(j + 1, sectors)
    left = lax.rem(j + sectors - 1, sectors)
    before = [(down, j), (i, left), (down, left)]
    after = [(up, j), (i, right), (up, right)]
    ranks = BLK // 4
    part = ranks * CAP
    k = lax.rem(j, ranks)
    a_peers = [lax.rem(k + o, ranks) for o in range(1, ranks)]
    b_peers = [lax.rem(i + o, sections) for o in range(1, sections)]
    c_peers = [lax.rem(j + o, sectors) for o in range(1, sectors)]
    myself = (i * sectors + j).astype(F32)

    loads = [pltpu.make_async_copy(src, dst, load_sem.at[n]) for n, (src, dst) in enumerate(
        [(pos, x_own), (vel, v_own), (rad, r_own), (pairs_in, pairs), (slots_in, slots),
         (home_in, home), (gas, g_own), (history, hist)])]
    for load in loads:
        load.start()
    barrier = pltpu.get_barrier_semaphore()
    peers = [(peer, j) for peer in b_peers] + [(i, peer) for peer in c_peers] + [before[2], after[2]]
    for peer in peers:
        pl.semaphore_signal(barrier, inc=1, device_id=peer, device_id_type=MESH)

    for load in loads[0:6]:
        load.wait()
    for t in range(3):
        ext[t, 0:BLK, :] = 100.0 * x_own[t]
        ext[3 + t, 0:BLK, :] = STEP_TIME * v_own[t]
    ext[6, 0:BLK, :] = 100.0 * r_own[...]
    for q in range(7):
        idle = 100.0 if q == 6 else 0.0
        ext[q, 4 * BLK:4 * BLK + 8, :] = jnp.full((8, PB), idle, F32)
        near_bc[BLK, q] = jnp.full((PB, PB), idle, F32)
    row = lax.broadcasted_iota(jnp.int32, (PB, 2 * PB), 0)
    side = lax.broadcasted_iota(jnp.int32, (PB, 2 * PB), 1) // PB

    def make_choice(p, _):
        choose[p] = ((row % BLK == 2 * p + side) & (row < 3 * BLK)).astype(F32).astype(BF16)
        return 0
    lax.fori_loop(0, BLK // 2, make_choice, 0)
    forces[1] = jnp.zeros((3, PB, PB), F32)

    tables[...] = jnp.zeros(tables.shape, jnp.int32)
    tables[0:2, 0:PAIRS] = pairs[...]
    tables[2:3, 0:PAIRS] = slots[...]
    place = lax.broadcasted_iota(jnp.int32, (PB, PB), 0)
    idle = BLK * 256 + 4 * BLK
    code = jnp.transpose(jnp.broadcast_to(tables[0:1, :] * 256 + tables[1:2, :] - idle, (PB, PB)))
    slot = jnp.transpose(jnp.broadcast_to(tables[2:3, :], (PB, PB)))
    active = (place < count[0, 0]) & (place < PAIRS)
    here = (slot == lax.broadcasted_iota(jnp.int32, (PB, PB), 1) % PAIRS) & active
    columns[...] = jnp.broadcast_to(idle + jnp.sum(jnp.where(here, code, 0), axis=0, keepdims=True), columns.shape)
    fetch = pltpu.make_async_copy(columns, codes, load_sem.at[8])
    fetch.start()
    pl.semaphore_wait(barrier, len(peers))

    def send(planes, sends, recvs):
        copies = []
        for n in range(3):
            copies.append(pltpu.make_async_remote_copy(
                src_ref=ext.at[planes, 0:BLK, :],
                dst_ref=ext.at[planes, (n + 1) * BLK:(n + 2) * BLK, :],
                send_sem=sends.at[n], recv_sem=recvs.at[n],
                device_id=before[n], device_id_type=MESH))
            copies[-1].start()
        return copies

    def spread(planes):
        for n, q in enumerate(planes):
            parts = [piece.astype(F32) for piece in split3(ext[q, 0:BLK, :])]
            stacked = jnp.concatenate(parts + [jnp.zeros((BLK, PB), F32)], axis=0)
            turned[pl.ds(n * PB, PB), :] = jnp.transpose(stacked).astype(BF16)

        def one(p, _):
            wide = jnp.dot(turned[0:len(planes) * PB, :], choose[p], preferred_element_type=F32)
            for n, q in enumerate(planes):
                near_bc[2 * p, q] = wide[n * PB:(n + 1) * PB, :PB]
                near_bc[2 * p + 1, q] = wide[n * PB:(n + 1) * PB, PB:]
            return 0
        lax.fori_loop(0, BLK // 2, one, 0)

    def two_pairs(p, _):
        near_sums(forces, pairs_f, 1, jnp.maximum(2 * p - 1, 0))
        contact(codes, ext, near_bc, hist, pairs_f, forces, 0, 2 * p)
        near_sums(forces, pairs_f, 0, 2 * p)
        contact(codes, ext, near_bc, hist, pairs_f, forces, 1, 2 * p + 1)
        return 0

    def sort_own():
        tables[3:4, 0:BLK] = home[...] + 1
        label = jnp.broadcast_to(tables[3:4, :].astype(F32), (PB, PB))
        target = jnp.floor((label - 1.0) * (1.0 / BLK))
        real = lax.broadcasted_iota(jnp.int32, (PB, PB), 1) < BLK
        rank_col = count_before((jnp.transpose(target) == target) & real)
        rank = jnp.transpose(rank_col)
        place_col = count_before((rank_col == rank) & (target != myself) & real)
        place = jnp.where((target != myself) & real, rank * CAP + jnp.transpose(place_col), -1.0)
        pick_a[...] = chosen_rows(place, BLK)
        return jnp.transpose(label)[0:BLK, :]

    def pack(pick, blocks_in, out):
        packed = exact_dot(pick, jnp.concatenate(blocks_in, axis=1))
        for t in range(len(blocks_in)):
            out[:, t, :] = packed[0:out.shape[0], t * PB:(t + 1) * PB]

    def hop_a(which, out, everything):
        copies = []
        for o, peer in enumerate(a_peers):
            copies.append(pltpu.make_async_remote_copy(
                src_ref=out.at[pl.ds(peer * CAP, CAP)],
                dst_ref=everything.at[pl.ds(i * part + k * CAP, CAP)],
                send_sem=a_send.at[which, o], recv_sem=a_recv.at[which, o],
                device_id=(i, j - k + peer), device_id_type=MESH))
            copies[-1].start()
        everything[pl.ds(i * part + k * CAP, CAP)] = out[pl.ds(k * CAP, CAP)]
        return copies

    def hop_b(which, everything):
        copies = []
        for o, peer in enumerate(b_peers):
            copies.append(pltpu.make_async_remote_copy(
                src_ref=everything.at[pl.ds(i * part, part)],
                dst_ref=everything.at[pl.ds(i * part, part)],
                send_sem=b_send.at[which, o], recv_sem=b_recv.at[which, o],
                device_id=(peer, j), device_id_type=MESH))
            copies[-1].start()
        return copies

    def sort_all():
        total = all_x.shape[0]
        label_col = all_x[:, 4, :]
        target_col = jnp.floor((label_col - 1.0) * (1.0 / BLK))
        target_row = jnp.concatenate([jnp.transpose(target_col)] * (total // PB), axis=0)
        target_wide = jnp.concatenate([target_col] * (total // PB), axis=1)
        place_col = count_before(target_wide == target_row)
        toward = target_col - (i * sectors).astype(F32)
        here = (toward >= 0.0) & (toward < float(sectors)) & (label_col > 0.0)
        pick_c[...] = chosen_rows(jnp.transpose(jnp.where(here, toward * CAP + place_col, -1.0)), sectors * CAP)

    def hop_c(which, out, come):
        copies = []
        for o, peer in enumerate(c_peers):
            copies.append(pltpu.make_async_remote_copy(
                src_ref=out.at[pl.ds(peer * CAP, CAP)],
                dst_ref=come.at[pl.ds(j * CAP, CAP)],
                send_sem=c_send.at[which, o], recv_sem=c_recv.at[which, o],
                device_id=(i, peer), device_id_type=MESH))
            copies[-1].start()
        come[pl.ds(j * CAP, CAP)] = out[pl.ds(j * CAP, CAP)]
        return copies

    def wait(copies):
        for copy in copies:
            copy.wait()

    def candidates(own, come):
        rest = jnp.zeros((PB - BLK - sectors * CAP, PB), F32)
        return [jnp.concatenate([mine, come[:, t, :], rest], axis=0) for t, mine in enumerate(own)]

    block = lax.broadcasted_iota(jnp.int32, (4 * BLK, PB), 0)
    lane = lax.broadcasted_iota(jnp.int32, (4 * BLK, PB), 1)
    code = jnp.broadcast_to(columns[0:1, :], (4 * BLK, PB))
    near = code // 256
    near = jnp.where(near < BLK, near, 4 * BLK)
    onehot = (jnp.where(lane < PAIRS, near, code % 256) == block).astype(F32)
    onehot = jnp.where(lane < PAIRS, onehot, -onehot).astype(BF16)
    mass = r_own[...] / 0.06
    mass = mass * mass * mass

    for substep in range(ITERS):
        last = substep == ITERS - 1
        if substep == 0:
            copies = send(slice(0, 7), first_send, first_recv)
        else:
            copies = send(slice(3, 6), halo_send, halo_recv)
        if last:
            early = [x_own[t] for t in range(3)] + [r_own[...], own_label]
            pack(pick_a[:, 0:BLK], early, out_x)
            first_hop = hop_a(0, out_x, all_x)
        spread(range(7) if substep == 0 else range(6))
        if substep == 0:
            own_label = sort_own()
            held = sections * part
            all_x[held:] = jnp.zeros((all_x.shape[0] - held,) + all_x.shape[1:], F32)
            all_v[held:] = jnp.zeros((all_v.shape[0] - held,) + all_v.shape[1:], F32)
        wait(copies)
        if substep == 0:
            wait(loads[6:])
            fetch.wait()
        else:
            for t in range(3):
                ext[t, BLK:4 * BLK, :] = ext[t, BLK:4 * BLK, :] + 100.0 * ext[3 + t, BLK:4 * BLK, :]

        if last:
            wait(first_hop)
            second_hop = hop_b(0, all_x)
            lax.fori_loop(0, FIRST_PART, two_pairs, 0)
            wait(second_hop)
            sort_all()
            pack(pick_c[...], [all_x[:, t, :] for t in range(5)], hand_x)
            third_hop = hop_c(0, hand_x, come_x)
            lax.fori_loop(FIRST_PART, PAIRS // 2, two_pairs, 0)
        else:
            lax.fori_loop(0, PAIRS // 2, two_pairs, 0)
        near_sums(forces, pairs_f, 1, PAIRS - 1)

        for t in range(3):
            acting[t] = exact_dot(onehot, pairs_f[t])
        returns = []
        for n in range(3):
            returns.append(pltpu.make_async_remote_copy(
                src_ref=acting.at[:, (n + 1) * BLK:(n + 2) * BLK, :],
                dst_ref=back.at[n],
                send_sem=back_send.at[n], recv_sem=back_recv.at[n],
                device_id=after[n], device_id_type=MESH))
            returns[-1].start()
        if last:
            wait(third_hop)
            both = candidates(early, come_x)
            pick_f[...] = chosen_rows(jnp.transpose(both[4] - 1.0 - myself * BLK), BLK)
            settled = exact_dot(pick_f[...], jnp.concatenate(both[0:4], axis=1))
            for t in range(3):
                x_out[t] = settled[:, t * PB:(t + 1) * PB]
            r_out[...] = settled[:, 3 * PB:4 * PB]
        wait(returns)
        for t in range(3):
            total = (acting[t, 0:BLK, :] + back[0, t] + back[1, t] + back[2, t]) * 10.0
            v = v_own[t]
            accel = total / mass + (g_own[t] - v) / 0.05
            if t == 1:
                accel = accel + GRAVITY_PULL
            v = v + STEP_TIME * accel
            v_own[t] = v
            if not last:
                x = x_own[t] + STEP_TIME * v
                x_own[t] = x
                ext[t, 0:BLK, :] = 100.0 * x
                ext[3 + t, 0:BLK, :] = STEP_TIME * v

    own = [v_own[t] for t in range(3)]
    pack(pick_a[:, 0:BLK], own, out_v)
    wait(hop_a(1, out_v, all_v))
    wait(hop_b(1, all_v))
    pack(pick_c[...], [all_v[:, t, :] for t in range(3)], hand_v)
    wait(hop_c(1, hand_v, come_v))
    settled = exact_dot(pick_f[...], jnp.concatenate(candidates(own, come_v), axis=1))
    for t in range(3):
        v = settled[:, t * PB:(t + 1) * PB]
        v_out[t] = v
        x_out[t] = x_out[t] + STEP_TIME * v


def substeps(sections, sectors, pairs, slots, count, home, pos, vel, rad, gas, history):
    vmem = pl.BlockSpec(memory_space=pltpu.VMEM)
    hbm = pl.BlockSpec(memory_space=pltpu.HBM)
    plane = jax.ShapeDtypeStruct((3, BLK, PB), F32)
    part = BLK // 4 * CAP
    total = -(-sections * part // PB) * PB
    three = pltpu.SemaphoreType.DMA((3,))
    hops = [pltpu.SemaphoreType.DMA((2, n)) for n in (BLK // 4 - 1, sections - 1, sectors - 1) for _ in range(2)]
    return pl.pallas_call(
        functools.partial(kernel, sections, sectors),
        out_shape=(plane, plane, jax.ShapeDtypeStruct((BLK, PB), F32), pltpu.VMEM(history.shape, F32)),
        in_specs=[hbm] * 8 + [pl.BlockSpec(memory_space=pltpu.SMEM)],
        out_specs=(vmem, vmem, vmem, vmem),
        scratch_shapes=[
            pltpu.VMEM((3, BLK, PB), F32),
            pltpu.VMEM((3, BLK, PB), F32),
            pltpu.VMEM((BLK, PB), F32),
            pltpu.VMEM((3, BLK, PB), F32),
            pltpu.VMEM(pairs.shape, jnp.int32),
            pltpu.VMEM(slots.shape, jnp.int32),
            pltpu.VMEM(home.shape, jnp.int32),
            pltpu.VMEM((8, PB), jnp.int32),
            pltpu.VMEM((8, PB), jnp.int32),
            pltpu.SMEM((8, PB), jnp.int32),
            pltpu.VMEM((7, 4 * BLK + 8, PB), F32),
            pltpu.VMEM((BLK + 1, 7, PB, PB), F32),
            pltpu.VMEM((BLK // 2, PB, 2 * PB), BF16),
            pltpu.VMEM((7 * PB, PB), BF16),
            pltpu.VMEM((2, 3, PB, PB), F32),
            pltpu.VMEM((3, 2 * PAIRS, PB), F32),
            pltpu.VMEM((3, 4 * BLK, PB), F32),
            pltpu.VMEM((3, 3, BLK, PB), F32),
            pltpu.VMEM((BLK, PB), BF16),
            pltpu.VMEM((sectors * CAP, total), BF16),
            pltpu.VMEM((BLK, PB), BF16),
        ] + [
            pltpu.VMEM((count, rows, PB), F32)
            for rows in (5, 3) for count in (part, total, sectors * CAP, sectors * CAP)
        ] + [pltpu.SemaphoreType.DMA((9,))] + [three] * 6 + hops,
        compiler_params=pltpu.CompilerParams(collective_id=0, has_side_effects=True, vmem_limit_bytes=32 << 20),
        name="substeps",
    )(*[pltpu.with_memory_space_constraint(a, pltpu.HBM)
        for a in (pairs, slots, home, pos, vel, rad, gas, history)], count)


def hand_over(x, v, r, hist, x_out, v_out, r_out, hist_out, sems):
    copies = [pltpu.make_async_copy(x, x_out, sems.at[0]),
              pltpu.make_async_copy(v, v_out, sems.at[1]),
              pltpu.make_async_copy(r, r_out, sems.at[2])]
    group = PAIRS // 8
    for n in range(8):
        rows = pl.ds(n * group, group)
        copies.append(pltpu.make_async_copy(hist.at[rows], hist_out.at[rows], sems.at[3 + n]))
    for copy in copies:
        copy.start()
    for copy in copies:
        copy.wait()


def results(x, v, r, hist):
    vmem = pl.BlockSpec(memory_space=pltpu.VMEM)
    hbm = pl.BlockSpec(memory_space=pl.ANY)
    return pl.pallas_call(
        hand_over,
        out_shape=tuple(jax.ShapeDtypeStruct(a.shape, F32) for a in (x, v, r, hist)),
        in_specs=[vmem] * 4,
        out_specs=(hbm,) * 4,
        scratch_shapes=[pltpu.SemaphoreType.DMA((11,))],
        compiler_params=pltpu.CompilerParams(vmem_limit_bytes=16 << 20),
        name="results",
    )(x, v, r, hist)


def local(
    positions,
    velocities,
    radius,
    gas_velocity,
    history,
    pair_list,
    history_slot,
    pair_count,
    new_home,
):
    def planes(array):
        return jnp.transpose(array[0, 0], (1, 0, 2))

    place, speed, radii, memory = results(*substeps(
        lax.axis_size("axial"), lax.axis_size("azim"), pair_list[0, 0], history_slot[0], pair_count, new_home[0],
        planes(positions), planes(velocities), radius[0, 0], planes(gas_velocity), history[0, 0]))
    return (
        jnp.transpose(place, (1, 0, 2))[None, None],
        jnp.transpose(speed, (1, 0, 2))[None, None],
        radii[None, None],
        memory[None, None],
    )


def solution(mesh):
    return jax.shard_map(
        local,
        mesh=mesh,
        in_specs=(
            P("axial", "azim", None, None, None),
            P("axial", "azim", None, None, None),
            P("axial", "azim", None, None),
            P("axial", "azim", None, None, None),
            P("axial", "azim", None, None, None, None),
            P("axial", "azim", None, None),
            P("axial", "azim", None),
            P("axial", "azim"),
            P("axial", "azim", None),
        ),
        out_specs=(
            P("axial", "azim", None, None, None),
            P("axial", "azim", None, None, None),
            P("axial", "azim", None, None),
            P("axial", "azim", None, None, None, None),
        ),
        check_vma=False,
    )
```

```python
import functools
import jax
import jax.numpy as jnp
from jax import lax
from jax.experimental import pallas as pl
from jax.experimental.pallas import tpu as pltpu
from jax.sharding import PartitionSpec as P

ITERS = 3
BLK = 32
PAIRS = 64
PB = 128
CAP = 3
TOGETHER = 8
FIRST_PART = 6
STEP_TIME = 0.01
GRAVITY_PULL = -9.81
MESH = pl.DeviceIdType.MESH
F32 = jnp.float32
BF16 = jnp.bfloat16


def split3(value):
    hi = value.astype(BF16)
    rest = value - hi.astype(F32)
    mid = rest.astype(BF16)
    lo = (rest - mid.astype(F32)).astype(BF16)
    return hi, mid, lo


def exact_dot(onehot, value):
    out = None
    for part in split3(value):
        term = jnp.dot(onehot, part, preferred_element_type=F32)
        out = term if out is None else out + term
    return out


def near_sums(forces, pairs_n, half, slot):
    for t in range(3):
        pairs_n[t, pl.ds(slot, 1), :] = jnp.sum(jnp.transpose(forces[half][t]), axis=0, keepdims=True)


def contact(codes, ext, near_bc, hist, pairs_f, forces, half, slot):
    code = codes[0, slot]
    a = code // 256
    c = code % 256
    far = [jnp.broadcast_to(ext[q, pl.ds(c, 1), :], (8, PB)) for q in range(7)]
    column = [None] * 3
    for k in range(16):
        r = slice(8 * k, 8 * k + 8)
        near = [near_bc[a, q, r, :] for q in range(7)]
        d = [near[q] - far[q] for q in range(3)]
        w = [near[q] - far[q] for q in range(3, 6)]
        d2 = jnp.maximum(d[0] * d[0] + d[1] * d[1] + d[2] * d[2], 1e-30)
        rs = lax.rsqrt(d2)
        inv = jnp.minimum(rs, 1.0)
        over = jnp.maximum(near[6] + far[6] - d2 * rs, 0.0)
        root = over * lax.rsqrt(jnp.maximum(over, 1e-30))
        q = (w[0] * d[0] + w[1] * d[1] + w[2] * d[2]) * (inv * inv)
        fade = jnp.minimum(over, 1.0)
        pull = root * (over * inv - 40.0 * q)
        drag = 80.0 * root
        for t in range(3):
            fresh = fade * (hist[slot, t, r, :] + (w[t] - q * d[t]))
            hist[slot, t, r, :] = fresh
            force = pull * d[t] - drag * fresh
            column[t] = force if column[t] is None else column[t] + force
            forces[half][t, r, :] = force
    for t in range(3):
        pairs_f[t, pl.ds(slot, 1), :] = jnp.sum(column[t], axis=0, keepdims=True)


def count_before(same):
    earlier = lax.broadcasted_iota(jnp.int32, same.shape, 1) < lax.broadcasted_iota(jnp.int32, same.shape, 0)
    marked = (same & earlier).astype(F32).astype(BF16)
    return jnp.dot(marked, jnp.ones((same.shape[1], PB), BF16), preferred_element_type=F32)


def chosen_rows(row_of, count):
    order = lax.broadcasted_iota(jnp.int32, (count, row_of.shape[1]), 0).astype(F32)
    return (row_of[0:count, :] == order).astype(F32).astype(BF16)


def kernel(sections, sectors, pairs_in, slots_in, home_in, pos, vel, rad, gas, history, count,
           x_out, v_out, r_out, hist,
           x_own, v_own, r_own, g_own, pairs, slots, home, tables, columns, codes,
           ext, near_bc, choose, turned, forces_even, forces_odd, pairs_n, pairs_f, acting, back,
           pick_a, pick_c, pick_f,
           out_x, all_x, hand_x, come_x, out_v, all_v, hand_v, come_v,
           load_sem, first_send, first_recv, halo_send, halo_recv, back_send, back_recv,
           a_send, a_recv, b_send, b_recv, c_send, c_recv):
    i = lax.axis_index("axial")
    j = lax.axis_index("azim")
    up = lax.rem(i + 1, sections)
    down = lax.rem(i + sections - 1, sections)
    right = lax.rem(j + 1, sectors)
    left = lax.rem(j + sectors - 1, sectors)
    before = [(down, j), (i, left), (down, left)]
    after = [(up, j), (i, right), (up, right)]
    ranks = BLK // 4
    part = ranks * CAP
    k = lax.rem(j, ranks)
    a_peers = [lax.rem(k + o, ranks) for o in range(1, ranks)]
    b_peers = [lax.rem(i + o, sections) for o in range(1, sections)]
    c_peers = [lax.rem(j + o, sectors) for o in range(1, sectors)]
    myself = (i * sectors + j).astype(F32)

    loads = [pltpu.make_async_copy(src, dst, load_sem.at[n]) for n, (src, dst) in enumerate(
        [(pos, x_own), (vel, v_own), (rad, r_own), (pairs_in, pairs), (slots_in, slots),
         (home_in, home), (gas, g_own), (history, hist)])]
    for load in loads:
        load.start()
    barrier = pltpu.get_barrier_semaphore()
    peers = [(peer, j) for peer in b_peers] + [(i, peer) for peer in c_peers] + [before[2], after[2]]
    for peer in peers:
        pl.semaphore_signal(barrier, inc=1, device_id=peer, device_id_type=MESH)

    for load in loads[0:6]:
        load.wait()
    for t in range(3):
        ext[t, 0:BLK, :] = 100.0 * x_own[t]
        ext[3 + t, 0:BLK, :] = STEP_TIME * v_own[t]
    ext[6, 0:BLK, :] = 100.0 * r_own[...]
    for q in range(7):
        idle = 100.0 if q == 6 else 0.0
        ext[q, 4 * BLK:4 * BLK + 8, :] = jnp.full((8, PB), idle, F32)
        near_bc[BLK, q] = jnp.full((PB, PB), idle, F32)
    row = lax.broadcasted_iota(jnp.int32, (PB, 2 * PB), 0)
    side = lax.broadcasted_iota(jnp.int32, (PB, 2 * PB), 1) // PB

    def make_choice(p, _):
        choose[p] = ((row % BLK == 2 * p + side) & (row < 3 * BLK)).astype(F32).astype(BF16)
        return 0
    lax.fori_loop(0, BLK // 2, make_choice, 0)
    forces = (forces_even, forces_odd)
    forces_odd[...] = jnp.zeros((3, PB, PB), F32)

    tables[...] = jnp.zeros(tables.shape, jnp.int32)
    tables[0:2, 0:PAIRS] = pairs[...]
    tables[2:3, 0:PAIRS] = slots[...]
    place = lax.broadcasted_iota(jnp.int32, (PB, PB), 0)
    idle = BLK * 256 + 4 * BLK
    code = jnp.transpose(jnp.broadcast_to(tables[0:1, :] * 256 + tables[1:2, :] - idle, (PB, PB)))
    slot = jnp.transpose(jnp.broadcast_to(tables[2:3, :], (PB, PB)))
    active = (place < count[0, 0]) & (place < PAIRS)
    here = (slot == lax.broadcasted_iota(jnp.int32, (PB, PB), 1) % PAIRS) & active
    columns[...] = jnp.broadcast_to(idle + jnp.sum(jnp.where(here, code, 0), axis=0, keepdims=True), columns.shape)
    fetch = pltpu.make_async_copy(columns, codes, load_sem.at[8])
    fetch.start()
    pl.semaphore_wait(barrier, len(peers))

    def send(planes, sends, recvs):
        copies = []
        for n in range(3):
            copies.append(pltpu.make_async_remote_copy(
                src_ref=ext.at[planes, 0:BLK, :],
                dst_ref=ext.at[planes, (n + 1) * BLK:(n + 2) * BLK, :],
                send_sem=sends.at[n], recv_sem=recvs.at[n],
                device_id=before[n], device_id_type=MESH))
            copies[-1].start()
        return copies

    def spread(planes):
        for n, q in enumerate(planes):
            parts = [piece.astype(F32) for piece in split3(ext[q, 0:BLK, :])]
            stacked = jnp.concatenate(parts + [jnp.zeros((BLK, PB), F32)], axis=0)
            turned[pl.ds(n * PB, PB), :] = jnp.transpose(stacked).astype(BF16)

        def one(p, _):
            wide = jnp.dot(turned[0:len(planes) * PB, :], choose[p], preferred_element_type=F32)
            for n, q in enumerate(planes):
                near_bc[2 * p, q] = wide[n * PB:(n + 1) * PB, :PB]
                near_bc[2 * p + 1, q] = wide[n * PB:(n + 1) * PB, PB:]
            return 0
        lax.fori_loop(0, BLK // 2, one, 0)

    def some_pairs(p, _):
        for n in range(TOGETHER):
            slot = TOGETHER * p + n
            near_sums(forces, pairs_n, (n + 1) % 2, jnp.maximum(slot - 1, 0))
            contact(codes, ext, near_bc, hist, pairs_f, forces, n % 2, slot)
        return 0

    def sort_own():
        tables[3:4, 0:BLK] = home[...] + 1
        label = jnp.broadcast_to(tables[3:4, :].astype(F32), (PB, PB))
        target = jnp.floor((label - 1.0) * (1.0 / BLK))
        real = lax.broadcasted_iota(jnp.int32, (PB, PB), 1) < BLK
        rank_col = count_before((jnp.transpose(target) == target) & real)
        rank = jnp.transpose(rank_col)
        place_col = count_before((rank_col == rank) & (target != myself) & real)
        place = jnp.where((target != myself) & real, rank * CAP + jnp.transpose(place_col), -1.0)
        pick_a[...] = chosen_rows(place, BLK)
        return jnp.transpose(label)[0:BLK, :]

    def pack(pick, blocks_in, out):
        packed = exact_dot(pick, jnp.concatenate(blocks_in, axis=1))
        for t in range(len(blocks_in)):
            out[:, t, :] = packed[0:out.shape[0], t * PB:(t + 1) * PB]

    def hop_a(which, out, everything):
        copies = []
        for o, peer in enumerate(a_peers):
            copies.append(pltpu.make_async_remote_copy(
                src_ref=out.at[pl.ds(peer * CAP, CAP)],
                dst_ref=everything.at[pl.ds(i * part + k * CAP, CAP)],
                send_sem=a_send.at[which, o], recv_sem=a_recv.at[which, o],
                device_id=(i, j - k + peer), device_id_type=MESH))
            copies[-1].start()
        everything[pl.ds(i * part + k * CAP, CAP)] = out[pl.ds(k * CAP, CAP)]
        return copies

    def hop_b(which, everything):
        copies = []
        for o, peer in enumerate(b_peers):
            copies.append(pltpu.make_async_remote_copy(
                src_ref=everything.at[pl.ds(i * part, part)],
                dst_ref=everything.at[pl.ds(i * part, part)],
                send_sem=b_send.at[which, o], recv_sem=b_recv.at[which, o],
                device_id=(peer, j), device_id_type=MESH))
            copies[-1].start()
        return copies

    def sort_all():
        total = all_x.shape[0]
        label_col = all_x[:, 4, :]
        target_col = jnp.floor((label_col - 1.0) * (1.0 / BLK))
        target_row = jnp.concatenate([jnp.transpose(target_col)] * (total // PB), axis=0)
        target_wide = jnp.concatenate([target_col] * (total // PB), axis=1)
        place_col = count_before(target_wide == target_row)
        toward = target_col - (i * sectors).astype(F32)
        here = (toward >= 0.0) & (toward < float(sectors)) & (label_col > 0.0)
        pick_c[...] = chosen_rows(jnp.transpose(jnp.where(here, toward * CAP + place_col, -1.0)), sectors * CAP)

    def hop_c(which, out, come):
        copies = []
        for o, peer in enumerate(c_peers):
            copies.append(pltpu.make_async_remote_copy(
                src_ref=out.at[pl.ds(peer * CAP, CAP)],
                dst_ref=come.at[pl.ds(j * CAP, CAP)],
                send_sem=c_send.at[which, o], recv_sem=c_recv.at[which, o],
                device_id=(i, peer), device_id_type=MESH))
            copies[-1].start()
        come[pl.ds(j * CAP, CAP)] = out[pl.ds(j * CAP, CAP)]
        return copies

    def wait(copies):
        for copy in copies:
            copy.wait()

    def candidates(own, come):
        rest = jnp.zeros((PB - BLK - sectors * CAP, PB), F32)
        return [jnp.concatenate([mine, come[:, t, :], rest], axis=0) for t, mine in enumerate(own)]

    block = lax.broadcasted_iota(jnp.int32, (4 * BLK, PB), 0)
    lane = lax.broadcasted_iota(jnp.int32, (4 * BLK, PB), 1)
    code = jnp.broadcast_to(columns[0:1, :], (4 * BLK, PB))
    near = code // 256
    near = jnp.where(near < BLK, near, 4 * BLK)
    onehot = (jnp.where(lane < PAIRS, near, code % 256) == block).astype(F32)
    onehot = jnp.where(lane < PAIRS, onehot, -onehot).astype(BF16)
    mass = r_own[...] / 0.06
    mass = mass * mass * mass

    for substep in range(ITERS):
        last = substep == ITERS - 1
        if substep == 0:
            copies = send(slice(0, 7), first_send, first_recv)
        else:
            copies = send(slice(3, 6), halo_send, halo_recv)
        if last:
            early = [x_own[t] for t in range(3)] + [r_own[...], own_label]
            pack(pick_a[:, 0:BLK], early, out_x)
            first_hop = hop_a(0, out_x, all_x)
        spread(range(7) if substep == 0 else range(6))
        if substep == 0:
            own_label = sort_own()
            held = sections * part
            all_x[held:] = jnp.zeros((all_x.shape[0] - held,) + all_x.shape[1:], F32)
            all_v[held:] = jnp.zeros((all_v.shape[0] - held,) + all_v.shape[1:], F32)
        wait(copies)
        if substep == 0:
            wait(loads[6:])
            fetch.wait()
        else:
            for t in range(3):
                ext[t, BLK:4 * BLK, :] = ext[t, BLK:4 * BLK, :] + 100.0 * ext[3 + t, BLK:4 * BLK, :]

        if last:
            wait(first_hop)
            second_hop = hop_b(0, all_x)
            lax.fori_loop(0, FIRST_PART, some_pairs, 0)
            wait(second_hop)
            sort_all()
            pack(pick_c[...], [all_x[:, t, :] for t in range(5)], hand_x)
            third_hop = hop_c(0, hand_x, come_x)
            lax.fori_loop(FIRST_PART, PAIRS // TOGETHER, some_pairs, 0)
        else:
            lax.fori_loop(0, PAIRS // TOGETHER, some_pairs, 0)
        near_sums(forces, pairs_n, 1, PAIRS - 1)

        for t in range(3):
            acting[t] = exact_dot(onehot, jnp.concatenate([pairs_n[t], pairs_f[t]], axis=0))
        returns = []
        for n in range(3):
            returns.append(pltpu.make_async_remote_copy(
                src_ref=acting.at[:, (n + 1) * BLK:(n + 2) * BLK, :],
                dst_ref=back.at[n],
                send_sem=back_send.at[n], recv_sem=back_recv.at[n],
                device_id=after[n], device_id_type=MESH))
            returns[-1].start()
        if last:
            wait(third_hop)
            both = candidates(early, come_x)
            pick_f[...] = chosen_rows(jnp.transpose(both[4] - 1.0 - myself * BLK), BLK)
            settled = exact_dot(pick_f[...], jnp.concatenate(both[0:4], axis=1))
            for t in range(3):
                x_out[t] = settled[:, t * PB:(t + 1) * PB]
            r_out[...] = settled[:, 3 * PB:4 * PB]
        wait(returns)
        for t in range(3):
            total = (acting[t, 0:BLK, :] + back[0, t] + back[1, t] + back[2, t]) * 10.0
            v = v_own[t]
            accel = total / mass + (g_own[t] - v) / 0.05
            if t == 1:
                accel = accel + GRAVITY_PULL
            v = v + STEP_TIME * accel
            v_own[t] = v
            if not last:
                x = x_own[t] + STEP_TIME * v
                x_own[t] = x
                ext[t, 0:BLK, :] = 100.0 * x
                ext[3 + t, 0:BLK, :] = STEP_TIME * v

    own = [v_own[t] for t in range(3)]
    pack(pick_a[:, 0:BLK], own, out_v)
    wait(hop_a(1, out_v, all_v))
    wait(hop_b(1, all_v))
    pack(pick_c[...], [all_v[:, t, :] for t in range(3)], hand_v)
    wait(hop_c(1, hand_v, come_v))
    settled = exact_dot(pick_f[...], jnp.concatenate(candidates(own, come_v), axis=1))
    for t in range(3):
        v = settled[:, t * PB:(t + 1) * PB]
        v_out[t] = v
        x_out[t] = x_out[t] + STEP_TIME * v


def substeps(sections, sectors, pairs, slots, count, home, pos, vel, rad, gas, history):
    vmem = pl.BlockSpec(memory_space=pltpu.VMEM)
    hbm = pl.BlockSpec(memory_space=pltpu.HBM)
    plane = jax.ShapeDtypeStruct((3, BLK, PB), F32)
    part = BLK // 4 * CAP
    total = -(-sections * part // PB) * PB
    three = pltpu.SemaphoreType.DMA((3,))
    hops = [pltpu.SemaphoreType.DMA((2, n)) for n in (BLK // 4 - 1, sections - 1, sectors - 1) for _ in range(2)]
    return pl.pallas_call(
        functools.partial(kernel, sections, sectors),
        out_shape=(plane, plane, jax.ShapeDtypeStruct((BLK, PB), F32), pltpu.VMEM(history.shape, F32)),
        in_specs=[hbm] * 8 + [pl.BlockSpec(memory_space=pltpu.SMEM)],
        out_specs=(vmem, vmem, vmem, vmem),
        scratch_shapes=[
            pltpu.VMEM((3, BLK, PB), F32),
            pltpu.VMEM((3, BLK, PB), F32),
            pltpu.VMEM((BLK, PB), F32),
            pltpu.VMEM((3, BLK, PB), F32),
            pltpu.VMEM(pairs.shape, jnp.int32),
            pltpu.VMEM(slots.shape, jnp.int32),
            pltpu.VMEM(home.shape, jnp.int32),
            pltpu.VMEM((8, PB), jnp.int32),
            pltpu.VMEM((8, PB), jnp.int32),
            pltpu.SMEM((8, PB), jnp.int32),
            pltpu.VMEM((7, 4 * BLK + 8, PB), F32),
            pltpu.VMEM((BLK + 1, 7, PB, PB), F32),
            pltpu.VMEM((BLK // 2, PB, 2 * PB), BF16),
            pltpu.VMEM((7 * PB, PB), BF16),
            pltpu.VMEM((3, PB, PB), F32),
            pltpu.VMEM((3, PB, PB), F32),
            pltpu.VMEM((3, PAIRS, PB), F32),
            pltpu.VMEM((3, PAIRS, PB), F32),
            pltpu.VMEM((3, 4 * BLK, PB), F32),
            pltpu.VMEM((3, 3, BLK, PB), F32),
            pltpu.VMEM((BLK, PB), BF16),
            pltpu.VMEM((sectors * CAP, total), BF16),
            pltpu.VMEM((BLK, PB), BF16),
        ] + [
            pltpu.VMEM((count, rows, PB), F32)
            for rows in (5, 3) for count in (part, total, sectors * CAP, sectors * CAP)
        ] + [pltpu.SemaphoreType.DMA((9,))] + [three] * 6 + hops,
        compiler_params=pltpu.CompilerParams(collective_id=0, has_side_effects=True, vmem_limit_bytes=32 << 20),
        name="substeps",
    )(*[pltpu.with_memory_space_constraint(a, pltpu.HBM)
        for a in (pairs, slots, home, pos, vel, rad, gas, history)], count)


def hand_over(x, v, r, hist, x_out, v_out, r_out, hist_out, sems):
    copies = [pltpu.make_async_copy(x, x_out, sems.at[0]),
              pltpu.make_async_copy(v, v_out, sems.at[1]),
              pltpu.make_async_copy(r, r_out, sems.at[2])]
    group = PAIRS // 8
    for n in range(8):
        rows = pl.ds(n * group, group)
        copies.append(pltpu.make_async_copy(hist.at[rows], hist_out.at[rows], sems.at[3 + n]))
    for copy in copies:
        copy.start()
    for copy in copies:
        copy.wait()


def results(x, v, r, hist):
    vmem = pl.BlockSpec(memory_space=pltpu.VMEM)
    hbm = pl.BlockSpec(memory_space=pl.ANY)
    return pl.pallas_call(
        hand_over,
        out_shape=tuple(jax.ShapeDtypeStruct(a.shape, F32) for a in (x, v, r, hist)),
        in_specs=[vmem] * 4,
        out_specs=(hbm,) * 4,
        scratch_shapes=[pltpu.SemaphoreType.DMA((11,))],
        compiler_params=pltpu.CompilerParams(vmem_limit_bytes=16 << 20),
        name="results",
    )(x, v, r, hist)


def local(
    positions,
    velocities,
    radius,
    gas_velocity,
    history,
    pair_list,
    history_slot,
    pair_count,
    new_home,
):
    def planes(array):
        return jnp.transpose(array[0, 0], (1, 0, 2))

    place, speed, radii, memory = results(*substeps(
        lax.axis_size("axial"), lax.axis_size("azim"), pair_list[0, 0], history_slot[0], pair_count, new_home[0],
        planes(positions), planes(velocities), radius[0, 0], planes(gas_velocity), history[0, 0]))
    return (
        jnp.transpose(place, (1, 0, 2))[None, None],
        jnp.transpose(speed, (1, 0, 2))[None, None],
        radii[None, None],
        memory[None, None],
    )


def solution(mesh):
    return jax.shard_map(
        local,
        mesh=mesh,
        in_specs=(
            P("axial", "azim", None, None, None),
            P("axial", "azim", None, None, None),
            P("axial", "azim", None, None),
            P("axial", "azim", None, None, None),
            P("axial", "azim", None, None, None, None),
            P("axial", "azim", None, None),
            P("axial", "azim", None),
            P("axial", "azim"),
            P("axial", "azim", None),
        ),
        out_specs=(
            P("axial", "azim", None, None, None),
            P("axial", "azim", None, None, None),
            P("axial", "azim", None, None),
            P("axial", "azim", None, None, None, None),
        ),
        check_vma=False,
    )
```

```python
import functools
import jax
import jax.numpy as jnp
from jax import lax
from jax.experimental import pallas as pl
from jax.experimental.pallas import tpu as pltpu
from jax.sharding import PartitionSpec as P

ITERS = 3
BLK = 32
PAIRS = 64
PB = 128
CAP = 3
TOGETHER = 8
FIRST_PART = 6
STEP_TIME = 0.01
GRAVITY_PULL = -9.81
MESH = pl.DeviceIdType.MESH
F32 = jnp.float32
BF16 = jnp.bfloat16


def split3(value):
    hi = value.astype(BF16)
    rest = value - hi.astype(F32)
    mid = rest.astype(BF16)
    lo = (rest - mid.astype(F32)).astype(BF16)
    return hi, mid, lo


def exact_dot(onehot, value):
    out = None
    for part in split3(value):
        term = jnp.dot(onehot, part, preferred_element_type=F32)
        out = term if out is None else out + term
    return out


def near_sums(forces, pairs_n, half, slot):
    for t in range(3):
        pairs_n[t, pl.ds(slot, 1), :] = jnp.sum(jnp.transpose(forces[half][t]), axis=0, keepdims=True)


def contact(codes, ext, near_bc, hist, pairs_f, forces, half, slot):
    code = codes[0, slot]
    a = code // 256
    c = code % 256
    far = [jnp.broadcast_to(ext[q, pl.ds(c, 1), :], (8, PB)) for q in range(7)]
    column = [None] * 3
    for k in range(16):
        r = slice(8 * k, 8 * k + 8)
        near = [near_bc[a, q, r, :] for q in range(7)]
        d = [near[q] - far[q] for q in range(3)]
        w = [near[q] - far[q] for q in range(3, 6)]
        d2 = jnp.maximum(d[0] * d[0] + d[1] * d[1] + d[2] * d[2], 1e-30)
        rs = lax.rsqrt(d2)
        inv = jnp.minimum(rs, 1.0)
        over = jnp.maximum(near[6] + far[6] - d2 * rs, 0.0)
        root = over * lax.rsqrt(jnp.maximum(over, 1e-30))
        q = (w[0] * d[0] + w[1] * d[1] + w[2] * d[2]) * (inv * inv)
        fade = jnp.minimum(over, 1.0)
        pull = root * (over * inv - 40.0 * q)
        drag = 80.0 * root
        for t in range(3):
            fresh = fade * (hist[slot, t, r, :] + (w[t] - q * d[t]))
            hist[slot, t, r, :] = fresh
            force = pull * d[t] - drag * fresh
            column[t] = force if column[t] is None else column[t] + force
            forces[half][t, r, :] = force
    for t in range(3):
        pairs_f[t, pl.ds(slot, 1), :] = jnp.sum(column[t], axis=0, keepdims=True)


def count_before(same):
    earlier = lax.broadcasted_iota(jnp.int32, same.shape, 1) < lax.broadcasted_iota(jnp.int32, same.shape, 0)
    marked = (same & earlier).astype(F32).astype(BF16)
    return jnp.dot(marked, jnp.ones((same.shape[1], PB), BF16), preferred_element_type=F32)


def chosen_rows(row_of, count):
    order = lax.broadcasted_iota(jnp.int32, (count, row_of.shape[1]), 0).astype(F32)
    return (row_of[0:count, :] == order).astype(F32).astype(BF16)


def kernel(sections, sectors, pairs_in, slots_in, home_in, pos, vel, rad, gas, history, count,
           x_out, v_out, r_out, hist,
           x_own, v_own, r_own, g_own, pairs, slots, home, tables, columns, codes,
           ext, near_bc, choose, turned, forces_even, forces_odd, pairs_n, pairs_f, acting, back,
           pick_a, pick_c, pick_f,
           out_x, all_x, hand_x, come_x, out_v, all_v, hand_v, come_v,
           load_sem, first_send, first_recv, halo_send, halo_recv, back_send, back_recv,
           a_send, a_recv, b_send, b_recv, c_send, c_recv):
    i = lax.axis_index("axial")
    j = lax.axis_index("azim")
    up = lax.rem(i + 1, sections)
    down = lax.rem(i + sections - 1, sections)
    right = lax.rem(j + 1, sectors)
    left = lax.rem(j + sectors - 1, sectors)
    before = [(down, j), (i, left), (down, left)]
    after = [(up, j), (i, right), (up, right)]
    ranks = BLK // 4
    part = ranks * CAP
    k = lax.rem(j, ranks)
    a_peers = [lax.rem(k + o, ranks) for o in range(1, ranks)]
    b_peers = [lax.rem(i + o, sections) for o in range(1, sections)]
    c_peers = [lax.rem(j + o, sectors) for o in range(1, sectors)]
    myself = (i * sectors + j).astype(F32)

    loads = [pltpu.make_async_copy(src, dst, load_sem.at[n]) for n, (src, dst) in enumerate(
        [(pos, x_own), (vel, v_own), (rad, r_own), (pairs_in, pairs), (slots_in, slots),
         (home_in, home), (gas, g_own), (history, hist)])]
    for load in loads:
        load.start()
    barrier = pltpu.get_barrier_semaphore()
    peers = [(peer, j) for peer in b_peers] + [(i, peer) for peer in c_peers] + [before[2], after[2]]
    for peer in peers:
        pl.semaphore_signal(barrier, inc=1, device_id=peer, device_id_type=MESH)

    for load in loads[0:6]:
        load.wait()
    for t in range(3):
        ext[t, 0:BLK, :] = 100.0 * x_own[t]
        ext[3 + t, 0:BLK, :] = STEP_TIME * v_own[t]
    ext[6, 0:BLK, :] = 100.0 * r_own[...]
    for q in range(7):
        idle = 100.0 if q == 6 else 0.0
        ext[q, 4 * BLK:4 * BLK + 8, :] = jnp.full((8, PB), idle, F32)
        near_bc[BLK, q] = jnp.full((PB, PB), idle, F32)
    row = lax.broadcasted_iota(jnp.int32, (PB, 2 * PB), 0)
    side = lax.broadcasted_iota(jnp.int32, (PB, 2 * PB), 1) // PB

    def make_choice(p, _):
        choose[p] = ((row % BLK == 2 * p + side) & (row < 3 * BLK)).astype(F32).astype(BF16)
        return 0
    lax.fori_loop(0, BLK // 2, make_choice, 0)
    forces = (forces_even, forces_odd)
    forces_odd[...] = jnp.zeros((3, PB, PB), F32)

    tables[...] = jnp.zeros(tables.shape, jnp.int32)
    tables[0:2, 0:PAIRS] = pairs[...]
    tables[2:3, 0:PAIRS] = slots[...]
    place = lax.broadcasted_iota(jnp.int32, (PB, PB), 0)
    idle = BLK * 256 + 4 * BLK
    code = jnp.transpose(jnp.broadcast_to(tables[0:1, :] * 256 + tables[1:2, :] - idle, (PB, PB)))
    slot = jnp.transpose(jnp.broadcast_to(tables[2:3, :], (PB, PB)))
    active = (place < count[0, 0]) & (place < PAIRS)
    here = (slot == lax.broadcasted_iota(jnp.int32, (PB, PB), 1) % PAIRS) & active
    columns[...] = jnp.broadcast_to(idle + jnp.sum(jnp.where(here, code, 0), axis=0, keepdims=True), columns.shape)
    fetch = pltpu.make_async_copy(columns, codes, load_sem.at[8])
    fetch.start()
    pl.semaphore_wait(barrier, len(peers))

    def send(planes, sends, recvs):
        copies = []
        for n in (2, 0, 1):
            copies.append(pltpu.make_async_remote_copy(
                src_ref=ext.at[planes, 0:BLK, :],
                dst_ref=ext.at[planes, (n + 1) * BLK:(n + 2) * BLK, :],
                send_sem=sends.at[n], recv_sem=recvs.at[n],
                device_id=before[n], device_id_type=MESH))
            copies[-1].start()
        return copies

    def spread(planes):
        for n, q in enumerate(planes):
            parts = [piece.astype(F32) for piece in split3(ext[q, 0:BLK, :])]
            stacked = jnp.concatenate(parts + [jnp.zeros((BLK, PB), F32)], axis=0)
            turned[pl.ds(n * PB, PB), :] = jnp.transpose(stacked).astype(BF16)

        def one(p, _):
            wide = jnp.dot(turned[0:len(planes) * PB, :], choose[p], preferred_element_type=F32)
            for n, q in enumerate(planes):
                near_bc[2 * p, q] = wide[n * PB:(n + 1) * PB, :PB]
                near_bc[2 * p + 1, q] = wide[n * PB:(n + 1) * PB, PB:]
            return 0
        lax.fori_loop(0, BLK // 2, one, 0)

    def some_pairs(p, _):
        for n in range(TOGETHER):
            slot = TOGETHER * p + n
            near_sums(forces, pairs_n, (n + 1) % 2, jnp.maximum(slot - 1, 0))
            contact(codes, ext, near_bc, hist, pairs_f, forces, n % 2, slot)
        return 0

    def sort_own():
        tables[3:4, 0:BLK] = home[...] + 1
        label = jnp.broadcast_to(tables[3:4, :].astype(F32), (PB, PB))
        target = jnp.floor((label - 1.0) * (1.0 / BLK))
        real = lax.broadcasted_iota(jnp.int32, (PB, PB), 1) < BLK
        rank_col = count_before((jnp.transpose(target) == target) & real)
        rank = jnp.transpose(rank_col)
        place_col = count_before((rank_col == rank) & (target != myself) & real)
        place = jnp.where((target != myself) & real, rank * CAP + jnp.transpose(place_col), -1.0)
        pick_a[...] = chosen_rows(place, BLK)
        return jnp.transpose(label)[0:BLK, :]

    def pack(pick, blocks_in, out):
        packed = exact_dot(pick, jnp.concatenate(blocks_in, axis=1))
        for t in range(len(blocks_in)):
            out[:, t, :] = packed[0:out.shape[0], t * PB:(t + 1) * PB]

    def hop_a(which, out, everything):
        copies = []
        for o, peer in enumerate(a_peers):
            copies.append(pltpu.make_async_remote_copy(
                src_ref=out.at[pl.ds(peer * CAP, CAP)],
                dst_ref=everything.at[pl.ds(i * part + k * CAP, CAP)],
                send_sem=a_send.at[which, o], recv_sem=a_recv.at[which, o],
                device_id=(i, j - k + peer), device_id_type=MESH))
            copies[-1].start()
        everything[pl.ds(i * part + k * CAP, CAP)] = out[pl.ds(k * CAP, CAP)]
        return copies

    def hop_b(which, everything):
        copies = []
        for o, peer in enumerate(b_peers):
            copies.append(pltpu.make_async_remote_copy(
                src_ref=everything.at[pl.ds(i * part, part)],
                dst_ref=everything.at[pl.ds(i * part, part)],
                send_sem=b_send.at[which, o], recv_sem=b_recv.at[which, o],
                device_id=(peer, j), device_id_type=MESH))
            copies[-1].start()
        return copies

    def sort_all():
        total = all_x.shape[0]
        label_col = all_x[:, 4, :]
        target_col = jnp.floor((label_col - 1.0) * (1.0 / BLK))
        target_row = jnp.concatenate([jnp.transpose(target_col)] * (total // PB), axis=0)
        target_wide = jnp.concatenate([target_col] * (total // PB), axis=1)
        place_col = count_before(target_wide == target_row)
        toward = target_col - (i * sectors).astype(F32)
        here = (toward >= 0.0) & (toward < float(sectors)) & (label_col > 0.0)
        pick_c[...] = chosen_rows(jnp.transpose(jnp.where(here, toward * CAP + place_col, -1.0)), sectors * CAP)

    def hop_c(which, out, come):
        copies = []
        for o, peer in enumerate(c_peers):
            copies.append(pltpu.make_async_remote_copy(
                src_ref=out.at[pl.ds(peer * CAP, CAP)],
                dst_ref=come.at[pl.ds(j * CAP, CAP)],
                send_sem=c_send.at[which, o], recv_sem=c_recv.at[which, o],
                device_id=(i, peer), device_id_type=MESH))
            copies[-1].start()
        come[pl.ds(j * CAP, CAP)] = out[pl.ds(j * CAP, CAP)]
        return copies

    def wait(copies):
        for copy in copies:
            copy.wait()

    def candidates(own, come):
        rest = jnp.zeros((PB - BLK - sectors * CAP, PB), F32)
        return [jnp.concatenate([mine, come[:, t, :], rest], axis=0) for t, mine in enumerate(own)]

    block = lax.broadcasted_iota(jnp.int32, (4 * BLK, PB), 0)
    lane = lax.broadcasted_iota(jnp.int32, (4 * BLK, PB), 1)
    code = jnp.broadcast_to(columns[0:1, :], (4 * BLK, PB))
    near = code // 256
    near = jnp.where(near < BLK, near, 4 * BLK)
    onehot = (jnp.where(lane < PAIRS, near, code % 256) == block).astype(F32)
    onehot = jnp.where(lane < PAIRS, onehot, -onehot).astype(BF16)
    mass = r_own[...] / 0.06
    mass = mass * mass * mass

    for substep in range(ITERS):
        last = substep == ITERS - 1
        if substep == 0:
            copies = send(slice(0, 7), first_send, first_recv)
        else:
            copies = send(slice(3, 6), halo_send, halo_recv)
        if last:
            early = [x_own[t] for t in range(3)] + [r_own[...], own_label]
            pack(pick_a[:, 0:BLK], early, out_x)
            first_hop = hop_a(0, out_x, all_x)
        spread(range(7) if substep == 0 else range(6))
        if substep == 0:
            own_label = sort_own()
            held = sections * part
            all_x[held:] = jnp.zeros((all_x.shape[0] - held,) + all_x.shape[1:], F32)
            all_v[held:] = jnp.zeros((all_v.shape[0] - held,) + all_v.shape[1:], F32)
        wait(copies)
        if substep == 0:
            wait(loads[6:])
            fetch.wait()
        else:
            for t in range(3):
                ext[t, BLK:4 * BLK, :] = ext[t, BLK:4 * BLK, :] + 100.0 * ext[3 + t, BLK:4 * BLK, :]

        if last:
            wait(first_hop)
            second_hop = hop_b(0, all_x)
            lax.fori_loop(0, FIRST_PART, some_pairs, 0)
            wait(second_hop)
            sort_all()
            pack(pick_c[...], [all_x[:, t, :] for t in range(5)], hand_x)
            third_hop = hop_c(0, hand_x, come_x)
            lax.fori_loop(FIRST_PART, PAIRS // TOGETHER, some_pairs, 0)
        else:
            lax.fori_loop(0, PAIRS // TOGETHER, some_pairs, 0)
        near_sums(forces, pairs_n, 1, PAIRS - 1)

        for t in range(3):
            acting[t] = exact_dot(onehot, jnp.concatenate([pairs_n[t], pairs_f[t]], axis=0))
        returns = []
        for n in (2, 0, 1):
            returns.append(pltpu.make_async_remote_copy(
                src_ref=acting.at[:, (n + 1) * BLK:(n + 2) * BLK, :],
                dst_ref=back.at[n],
                send_sem=back_send.at[n], recv_sem=back_recv.at[n],
                device_id=after[n], device_id_type=MESH))
            returns[-1].start()
        if last:
            wait(third_hop)
            both = candidates(early, come_x)
            pick_f[...] = chosen_rows(jnp.transpose(both[4] - 1.0 - myself * BLK), BLK)
            settled = exact_dot(pick_f[...], jnp.concatenate(both[0:4], axis=1))
            for t in range(3):
                x_out[t] = settled[:, t * PB:(t + 1) * PB]
            r_out[...] = settled[:, 3 * PB:4 * PB]
        wait(returns)
        for t in range(3):
            total = (acting[t, 0:BLK, :] + back[0, t] + back[1, t] + back[2, t]) * 10.0
            v = v_own[t]
            accel = total / mass + (g_own[t] - v) / 0.05
            if t == 1:
                accel = accel + GRAVITY_PULL
            v = v + STEP_TIME * accel
            v_own[t] = v
            if not last:
                x = x_own[t] + STEP_TIME * v
                x_own[t] = x
                ext[t, 0:BLK, :] = 100.0 * x
                ext[3 + t, 0:BLK, :] = STEP_TIME * v

    own = [v_own[t] for t in range(3)]
    pack(pick_a[:, 0:BLK], own, out_v)
    wait(hop_a(1, out_v, all_v))
    wait(hop_b(1, all_v))
    pack(pick_c[...], [all_v[:, t, :] for t in range(3)], hand_v)
    wait(hop_c(1, hand_v, come_v))
    settled = exact_dot(pick_f[...], jnp.concatenate(candidates(own, come_v), axis=1))
    for t in range(3):
        v = settled[:, t * PB:(t + 1) * PB]
        v_out[t] = v
        x_out[t] = x_out[t] + STEP_TIME * v


def substeps(sections, sectors, pairs, slots, count, home, pos, vel, rad, gas, history):
    vmem = pl.BlockSpec(memory_space=pltpu.VMEM)
    hbm = pl.BlockSpec(memory_space=pltpu.HBM)
    plane = jax.ShapeDtypeStruct((3, BLK, PB), F32)
    part = BLK // 4 * CAP
    total = -(-sections * part // PB) * PB
    three = pltpu.SemaphoreType.DMA((3,))
    hops = [pltpu.SemaphoreType.DMA((2, n)) for n in (BLK // 4 - 1, sections - 1, sectors - 1) for _ in range(2)]
    return pl.pallas_call(
        functools.partial(kernel, sections, sectors),
        out_shape=(plane, plane, jax.ShapeDtypeStruct((BLK, PB), F32), pltpu.VMEM(history.shape, F32)),
        in_specs=[hbm] * 8 + [pl.BlockSpec(memory_space=pltpu.SMEM)],
        out_specs=(vmem, vmem, vmem, vmem),
        scratch_shapes=[
            pltpu.VMEM((3, BLK, PB), F32),
            pltpu.VMEM((3, BLK, PB), F32),
            pltpu.VMEM((BLK, PB), F32),
            pltpu.VMEM((3, BLK, PB), F32),
            pltpu.VMEM(pairs.shape, jnp.int32),
            pltpu.VMEM(slots.shape, jnp.int32),
            pltpu.VMEM(home.shape, jnp.int32),
            pltpu.VMEM((8, PB), jnp.int32),
            pltpu.VMEM((8, PB), jnp.int32),
            pltpu.SMEM((8, PB), jnp.int32),
            pltpu.VMEM((7, 4 * BLK + 8, PB), F32),
            pltpu.VMEM((BLK + 1, 7, PB, PB), F32),
            pltpu.VMEM((BLK // 2, PB, 2 * PB), BF16),
            pltpu.VMEM((7 * PB, PB), BF16),
            pltpu.VMEM((3, PB, PB), F32),
            pltpu.VMEM((3, PB, PB), F32),
            pltpu.VMEM((3, PAIRS, PB), F32),
            pltpu.VMEM((3, PAIRS, PB), F32),
            pltpu.VMEM((3, 4 * BLK, PB), F32),
            pltpu.VMEM((3, 3, BLK, PB), F32),
            pltpu.VMEM((BLK, PB), BF16),
            pltpu.VMEM((sectors * CAP, total), BF16),
            pltpu.VMEM((BLK, PB), BF16),
        ] + [
            pltpu.VMEM((count, rows, PB), F32)
            for rows in (5, 3) for count in (part, total, sectors * CAP, sectors * CAP)
        ] + [pltpu.SemaphoreType.DMA((9,))] + [three] * 6 + hops,
        compiler_params=pltpu.CompilerParams(collective_id=0, has_side_effects=True, vmem_limit_bytes=32 << 20),
        name="substeps",
    )(*[pltpu.with_memory_space_constraint(a, pltpu.HBM)
        for a in (pairs, slots, home, pos, vel, rad, gas, history)], count)


def hand_over(x, v, r, hist, x_out, v_out, r_out, hist_out, sems):
    copies = [pltpu.make_async_copy(x, x_out, sems.at[0]),
              pltpu.make_async_copy(v, v_out, sems.at[1]),
              pltpu.make_async_copy(r, r_out, sems.at[2])]
    group = PAIRS // 8
    for n in range(8):
        rows = pl.ds(n * group, group)
        copies.append(pltpu.make_async_copy(hist.at[rows], hist_out.at[rows], sems.at[3 + n]))
    for copy in copies:
        copy.start()
    for copy in copies:
        copy.wait()


def results(x, v, r, hist):
    vmem = pl.BlockSpec(memory_space=pltpu.VMEM)
    hbm = pl.BlockSpec(memory_space=pl.ANY)
    return pl.pallas_call(
        hand_over,
        out_shape=tuple(jax.ShapeDtypeStruct(a.shape, F32) for a in (x, v, r, hist)),
        in_specs=[vmem] * 4,
        out_specs=(hbm,) * 4,
        scratch_shapes=[pltpu.SemaphoreType.DMA((11,))],
        compiler_params=pltpu.CompilerParams(vmem_limit_bytes=16 << 20),
        name="results",
    )(x, v, r, hist)


def local(
    positions,
    velocities,
    radius,
    gas_velocity,
    history,
    pair_list,
    history_slot,
    pair_count,
    new_home,
):
    def planes(array):
        return jnp.transpose(array[0, 0], (1, 0, 2))

    place, speed, radii, memory = results(*substeps(
        lax.axis_size("axial"), lax.axis_size("azim"), pair_list[0, 0], history_slot[0], pair_count, new_home[0],
        planes(positions), planes(velocities), radius[0, 0], planes(gas_velocity), history[0, 0]))
    return (
        jnp.transpose(place, (1, 0, 2))[None, None],
        jnp.transpose(speed, (1, 0, 2))[None, None],
        radii[None, None],
        memory[None, None],
    )


def solution(mesh):
    return jax.shard_map(
        local,
        mesh=mesh,
        in_specs=(
            P("axial", "azim", None, None, None),
            P("axial", "azim", None, None, None),
            P("axial", "azim", None, None),
            P("axial", "azim", None, None, None),
            P("axial", "azim", None, None, None, None),
            P("axial", "azim", None, None),
            P("axial", "azim", None),
            P("axial", "azim"),
            P("axial", "azim", None),
        ),
        out_specs=(
            P("axial", "azim", None, None, None),
            P("axial", "azim", None, None, None),
            P("axial", "azim", None, None),
            P("axial", "azim", None, None, None, None),
        ),
        check_vma=False,
    )
```

```python
import functools
import jax
import jax.numpy as jnp
from jax import lax
from jax.experimental import pallas as pl
from jax.experimental.pallas import tpu as pltpu
from jax.sharding import PartitionSpec as P

ITERS = 3
BLK = 32
PAIRS = 64
PB = 128
CAP = 3
TOGETHER = 8
FIRST_PART = 6
STEP_TIME = 0.01
GRAVITY_PULL = -9.81
MESH = pl.DeviceIdType.MESH
F32 = jnp.float32
BF16 = jnp.bfloat16


def split3(value):
    hi = value.astype(BF16)
    rest = value - hi.astype(F32)
    mid = rest.astype(BF16)
    lo = (rest - mid.astype(F32)).astype(BF16)
    return hi, mid, lo


def exact_dot(onehot, value):
    out = None
    for part in split3(value):
        term = jnp.dot(onehot, part, preferred_element_type=F32)
        out = term if out is None else out + term
    return out


def near_sums(forces, pairs_n, half, slot):
    for t in range(3):
        pairs_n[t, pl.ds(slot, 1), :] = jnp.sum(jnp.transpose(forces[half][t]), axis=0, keepdims=True)


def contact(codes, ext, near_bc, hist, pairs_f, forces, half, slot):
    code = codes[0, slot]
    a = code // 256
    c = code % 256
    far = [jnp.broadcast_to(ext[q, pl.ds(c, 1), :], (8, PB)) for q in range(7)]
    column = [None] * 3
    for k in range(16):
        r = slice(8 * k, 8 * k + 8)
        near = [near_bc[a, q, r, :] for q in range(7)]
        d = [near[q] - far[q] for q in range(3)]
        w = [near[q] - far[q] for q in range(3, 6)]
        d2 = jnp.maximum(d[0] * d[0] + d[1] * d[1] + d[2] * d[2], 1e-30)
        rs = lax.rsqrt(d2)
        inv = jnp.minimum(rs, 1.0)
        over = jnp.maximum(near[6] + far[6] - d2 * rs, 0.0)
        root = over * lax.rsqrt(jnp.maximum(over, 1e-30))
        q = (w[0] * d[0] + w[1] * d[1] + w[2] * d[2]) * (inv * inv)
        fade = jnp.minimum(over, 1.0)
        pull = root * (over * inv - 40.0 * q)
        drag = 80.0 * root
        for t in range(3):
            fresh = fade * (hist[slot, t, r, :] + (w[t] - q * d[t]))
            hist[slot, t, r, :] = fresh
            force = pull * d[t] - drag * fresh
            column[t] = force if column[t] is None else column[t] + force
            forces[half][t, r, :] = force
    for t in range(3):
        pairs_f[t, pl.ds(slot, 1), :] = jnp.sum(column[t], axis=0, keepdims=True)


def count_before(same):
    earlier = lax.broadcasted_iota(jnp.int32, same.shape, 1) < lax.broadcasted_iota(jnp.int32, same.shape, 0)
    marked = (same & earlier).astype(F32).astype(BF16)
    return jnp.dot(marked, jnp.ones((same.shape[1], PB), BF16), preferred_element_type=F32)


def chosen_rows(row_of, count):
    order = lax.broadcasted_iota(jnp.int32, (count, row_of.shape[1]), 0).astype(F32)
    return (row_of[0:count, :] == order).astype(F32).astype(BF16)


def kernel(sections, sectors, pairs_in, slots_in, home_in, pos, vel, rad, gas, history, count,
           x_out, v_out, r_out, hist,
           x_own, v_own, r_own, g_own, pairs, slots, home, tables, columns, codes,
           ext, near_bc, choose, turned, forces_even, forces_odd, pairs_n, pairs_f, acting, back,
           pick_a, pick_c, pick_f,
           out_x, all_x, hand_x, come_x, out_v, all_v, hand_v, come_v,
           load_sem, first_send, first_recv, halo_send, halo_recv, back_send, back_recv,
           a_send, a_recv, b_send, b_recv, c_send, c_recv):
    i = lax.axis_index("axial")
    j = lax.axis_index("azim")
    up = lax.rem(i + 1, sections)
    down = lax.rem(i + sections - 1, sections)
    right = lax.rem(j + 1, sectors)
    left = lax.rem(j + sectors - 1, sectors)
    before = [(down, j), (i, left), (down, left)]
    after = [(up, j), (i, right), (up, right)]
    ranks = BLK // 4
    part = ranks * CAP
    k = lax.rem(j, ranks)
    a_peers = [lax.rem(k + o, ranks) for o in range(1, ranks)]
    b_peers = [lax.rem(i + o, sections) for o in range(1, sections)]
    c_peers = [lax.rem(j + o, sectors) for o in range(1, sectors)]
    myself = (i * sectors + j).astype(F32)

    loads = [pltpu.make_async_copy(src, dst, load_sem.at[n]) for n, (src, dst) in enumerate(
        [(pos, x_own), (vel, v_own), (rad, r_own), (pairs_in, pairs), (slots_in, slots),
         (home_in, home), (gas, g_own), (history, hist)])]
    for load in loads:
        load.start()
    barrier = pltpu.get_barrier_semaphore()
    peers = [(peer, j) for peer in b_peers] + [(i, peer) for peer in c_peers] + [before[2], after[2]]
    for peer in peers:
        pl.semaphore_signal(barrier, inc=1, device_id=peer, device_id_type=MESH)

    for load in loads[0:6]:
        load.wait()
    for t in range(3):
        ext[t, 0:BLK, :] = 100.0 * x_own[t]
        ext[3 + t, 0:BLK, :] = STEP_TIME * v_own[t]
    ext[6, 0:BLK, :] = 100.0 * r_own[...]
    for q in range(7):
        idle = 100.0 if q == 6 else 0.0
        ext[q, 4 * BLK:4 * BLK + 8, :] = jnp.full((8, PB), idle, F32)
        near_bc[BLK, q] = jnp.full((PB, PB), idle, F32)
    row = lax.broadcasted_iota(jnp.int32, (PB, 2 * PB), 0)
    side = lax.broadcasted_iota(jnp.int32, (PB, 2 * PB), 1) // PB

    def make_choice(p, _):
        choose[p] = ((row % BLK == 2 * p + side) & (row < 3 * BLK)).astype(F32).astype(BF16)
        return 0
    lax.fori_loop(0, BLK // 2, make_choice, 0)
    forces = (forces_even, forces_odd)
    forces_odd[...] = jnp.zeros((3, PB, PB), F32)

    tables[...] = jnp.zeros(tables.shape, jnp.int32)
    tables[0:2, 0:PAIRS] = pairs[...]
    tables[2:3, 0:PAIRS] = slots[...]
    place = lax.broadcasted_iota(jnp.int32, (PB, PB), 0)
    idle = BLK * 256 + 4 * BLK
    code = jnp.transpose(jnp.broadcast_to(tables[0:1, :] * 256 + tables[1:2, :] - idle, (PB, PB)))
    slot = jnp.transpose(jnp.broadcast_to(tables[2:3, :], (PB, PB)))
    active = (place < count[0, 0]) & (place < PAIRS)
    here = (slot == lax.broadcasted_iota(jnp.int32, (PB, PB), 1) % PAIRS) & active
    columns[...] = jnp.broadcast_to(idle + jnp.sum(jnp.where(here, code, 0), axis=0, keepdims=True), columns.shape)
    fetch = pltpu.make_async_copy(columns, codes, load_sem.at[8])
    fetch.start()
    pl.semaphore_wait(barrier, len(peers))

    def send(planes, sends, recvs):
        copies = []
        for n in range(3):
            copies.append(pltpu.make_async_remote_copy(
                src_ref=ext.at[planes, 0:BLK, :],
                dst_ref=ext.at[planes, (n + 1) * BLK:(n + 2) * BLK, :],
                send_sem=sends.at[n], recv_sem=recvs.at[n],
                device_id=before[n], device_id_type=MESH))
            copies[-1].start()
        return copies

    def spread(planes):
        for n, q in enumerate(planes):
            parts = [piece.astype(F32) for piece in split3(ext[q, 0:BLK, :])]
            stacked = jnp.concatenate(parts + [jnp.zeros((BLK, PB), F32)], axis=0)
            turned[pl.ds(n * PB, PB), :] = jnp.transpose(stacked).astype(BF16)

        def one(p, _):
            wide = jnp.dot(turned[0:len(planes) * PB, :], choose[p], preferred_element_type=F32)
            for n, q in enumerate(planes):
                near_bc[2 * p, q] = wide[n * PB:(n + 1) * PB, :PB]
                near_bc[2 * p + 1, q] = wide[n * PB:(n + 1) * PB, PB:]
            return 0
        lax.fori_loop(0, BLK // 2, one, 0)

    def some_pairs(p, _):
        for n in range(TOGETHER):
            slot = TOGETHER * p + n
            near_sums(forces, pairs_n, (n + 1) % 2, jnp.maximum(slot - 1, 0))
            contact(codes, ext, near_bc, hist, pairs_f, forces, n % 2, slot)
        return 0

    def sort_own():
        tables[3:4, 0:BLK] = home[...] + 1
        label = jnp.broadcast_to(tables[3:4, :].astype(F32), (PB, PB))
        target = jnp.floor((label - 1.0) * (1.0 / BLK))
        real = lax.broadcasted_iota(jnp.int32, (PB, PB), 1) < BLK
        rank_col = count_before((jnp.transpose(target) == target) & real)
        rank = jnp.transpose(rank_col)
        place_col = count_before((rank_col == rank) & (target != myself) & real)
        place = jnp.where((target != myself) & real, rank * CAP + jnp.transpose(place_col), -1.0)
        pick_a[...] = chosen_rows(place, BLK)
        return jnp.transpose(label)[0:BLK, :]

    def pack(pick, blocks_in, out):
        packed = exact_dot(pick, jnp.concatenate(blocks_in, axis=1))
        for t in range(len(blocks_in)):
            out[:, t, :] = packed[0:out.shape[0], t * PB:(t + 1) * PB]

    def hop_a(which, out, everything):
        copies = []
        for o, peer in enumerate(a_peers):
            copies.append(pltpu.make_async_remote_copy(
                src_ref=out.at[pl.ds(peer * CAP, CAP)],
                dst_ref=everything.at[pl.ds(i * part + k * CAP, CAP)],
                send_sem=a_send.at[which, o], recv_sem=a_recv.at[which, o],
                device_id=(i, j - k + peer), device_id_type=MESH))
            copies[-1].start()
        everything[pl.ds(i * part + k * CAP, CAP)] = out[pl.ds(k * CAP, CAP)]
        return copies

    def hop_b(which, everything):
        copies = []
        for o, peer in enumerate(b_peers):
            copies.append(pltpu.make_async_remote_copy(
                src_ref=everything.at[pl.ds(i * part, part)],
                dst_ref=everything.at[pl.ds(i * part, part)],
                send_sem=b_send.at[which, o], recv_sem=b_recv.at[which, o],
                device_id=(peer, j), device_id_type=MESH))
            copies[-1].start()
        return copies

    def sort_all():
        total = all_x.shape[0]
        label_col = all_x[:, 4, :]
        target_col = jnp.floor((label_col - 1.0) * (1.0 / BLK))
        target_row = jnp.concatenate([jnp.transpose(target_col)] * (total // PB), axis=0)
        target_wide = jnp.concatenate([target_col] * (total // PB), axis=1)
        place_col = count_before(target_wide == target_row)
        toward = target_col - (i * sectors).astype(F32)
        here = (toward >= 0.0) & (toward < float(sectors)) & (label_col > 0.0)
        pick_c[...] = chosen_rows(jnp.transpose(jnp.where(here, toward * CAP + place_col, -1.0)), sectors * CAP)

    def hop_c(which, out, come):
        copies = []
        for o, peer in enumerate(c_peers):
            copies.append(pltpu.make_async_remote_copy(
                src_ref=out.at[pl.ds(peer * CAP, CAP)],
                dst_ref=come.at[pl.ds(j * CAP, CAP)],
                send_sem=c_send.at[which, o], recv_sem=c_recv.at[which, o],
                device_id=(i, peer), device_id_type=MESH))
            copies[-1].start()
        come[pl.ds(j * CAP, CAP)] = out[pl.ds(j * CAP, CAP)]
        return copies

    def wait(copies):
        for copy in copies:
            copy.wait()

    def candidates(own, come):
        rest = jnp.zeros((PB - BLK - sectors * CAP, PB), F32)
        return [jnp.concatenate([mine, come[:, t, :], rest], axis=0) for t, mine in enumerate(own)]

    block = lax.broadcasted_iota(jnp.int32, (4 * BLK, PB), 0)
    lane = lax.broadcasted_iota(jnp.int32, (4 * BLK, PB), 1)
    code = jnp.broadcast_to(columns[0:1, :], (4 * BLK, PB))
    near = code // 256
    near = jnp.where(near < BLK, near, 4 * BLK)
    onehot = (jnp.where(lane < PAIRS, near, code % 256) == block).astype(F32)
    onehot = jnp.where(lane < PAIRS, onehot, -onehot).astype(BF16)
    mass = r_own[...] / 0.06
    mass = mass * mass * mass

    for substep in range(ITERS):
        last = substep == ITERS - 1
        if substep == 0:
            copies = send(slice(0, 7), first_send, first_recv)
        else:
            copies = send(slice(3, 6), halo_send, halo_recv)
        if last:
            early = [x_own[t] for t in range(3)] + [r_own[...], own_label]
            pack(pick_a[:, 0:BLK], early, out_x)
            first_hop = hop_a(0, out_x, all_x)
        spread(range(7) if substep == 0 else range(6))
        if substep == 0:
            own_label = sort_own()
            held = sections * part
            all_x[held:] = jnp.zeros((all_x.shape[0] - held,) + all_x.shape[1:], F32)
            all_v[held:] = jnp.zeros((all_v.shape[0] - held,) + all_v.shape[1:], F32)
        wait(copies)
        if substep == 0:
            wait(loads[6:])
            fetch.wait()
        else:
            for t in range(3):
                ext[t, BLK:4 * BLK, :] = ext[t, BLK:4 * BLK, :] + 100.0 * ext[3 + t, BLK:4 * BLK, :]

        if last:
            wait(first_hop)
            second_hop = hop_b(0, all_x)
            lax.fori_loop(0, FIRST_PART, some_pairs, 0)
            wait(second_hop)
            sort_all()
            pack(pick_c[...], [all_x[:, t, :] for t in range(5)], hand_x)
            third_hop = hop_c(0, hand_x, come_x)
            lax.fori_loop(FIRST_PART, PAIRS // TOGETHER, some_pairs, 0)
        else:
            lax.fori_loop(0, PAIRS // TOGETHER, some_pairs, 0)
        near_sums(forces, pairs_n, 1, PAIRS - 1)

        returns = []
        for t in range(3):
            acting[t] = exact_dot(onehot, jnp.concatenate([pairs_n[t], pairs_f[t]], axis=0))
            for n in (2, 0, 1):
                returns.append(pltpu.make_async_remote_copy(
                    src_ref=acting.at[t, (n + 1) * BLK:(n + 2) * BLK, :],
                    dst_ref=back.at[n, t],
                    send_sem=back_send.at[n, t], recv_sem=back_recv.at[n, t],
                    device_id=after[n], device_id_type=MESH))
                returns[-1].start()
        if last:
            wait(third_hop)
            both = candidates(early, come_x)
            pick_f[...] = chosen_rows(jnp.transpose(both[4] - 1.0 - myself * BLK), BLK)
            settled = exact_dot(pick_f[...], jnp.concatenate(both[0:4], axis=1))
            for t in range(3):
                x_out[t] = settled[:, t * PB:(t + 1) * PB]
            r_out[...] = settled[:, 3 * PB:4 * PB]
        wait(returns)
        for t in range(3):
            total = (acting[t, 0:BLK, :] + back[0, t] + back[1, t] + back[2, t]) * 10.0
            v = v_own[t]
            accel = total / mass + (g_own[t] - v) / 0.05
            if t == 1:
                accel = accel + GRAVITY_PULL
            v = v + STEP_TIME * accel
            v_own[t] = v
            if not last:
                x = x_own[t] + STEP_TIME * v
                x_own[t] = x
                ext[t, 0:BLK, :] = 100.0 * x
                ext[3 + t, 0:BLK, :] = STEP_TIME * v

    own = [v_own[t] for t in range(3)]
    pack(pick_a[:, 0:BLK], own, out_v)
    wait(hop_a(1, out_v, all_v))
    wait(hop_b(1, all_v))
    pack(pick_c[...], [all_v[:, t, :] for t in range(3)], hand_v)
    wait(hop_c(1, hand_v, come_v))
    settled = exact_dot(pick_f[...], jnp.concatenate(candidates(own, come_v), axis=1))
    for t in range(3):
        v = settled[:, t * PB:(t + 1) * PB]
        v_out[t] = v
        x_out[t] = x_out[t] + STEP_TIME * v


def substeps(sections, sectors, pairs, slots, count, home, pos, vel, rad, gas, history):
    vmem = pl.BlockSpec(memory_space=pltpu.VMEM)
    hbm = pl.BlockSpec(memory_space=pltpu.HBM)
    plane = jax.ShapeDtypeStruct((3, BLK, PB), F32)
    part = BLK // 4 * CAP
    total = -(-sections * part // PB) * PB
    three = pltpu.SemaphoreType.DMA((3,))
    hops = [pltpu.SemaphoreType.DMA((2, n)) for n in (BLK // 4 - 1, sections - 1, sectors - 1) for _ in range(2)]
    return pl.pallas_call(
        functools.partial(kernel, sections, sectors),
        out_shape=(plane, plane, jax.ShapeDtypeStruct((BLK, PB), F32), pltpu.VMEM(history.shape, F32)),
        in_specs=[hbm] * 8 + [pl.BlockSpec(memory_space=pltpu.SMEM)],
        out_specs=(vmem, vmem, vmem, vmem),
        scratch_shapes=[
            pltpu.VMEM((3, BLK, PB), F32),
            pltpu.VMEM((3, BLK, PB), F32),
            pltpu.VMEM((BLK, PB), F32),
            pltpu.VMEM((3, BLK, PB), F32),
            pltpu.VMEM(pairs.shape, jnp.int32),
            pltpu.VMEM(slots.shape, jnp.int32),
            pltpu.VMEM(home.shape, jnp.int32),
            pltpu.VMEM((8, PB), jnp.int32),
            pltpu.VMEM((8, PB), jnp.int32),
            pltpu.SMEM((8, PB), jnp.int32),
            pltpu.VMEM((7, 4 * BLK + 8, PB), F32),
            pltpu.VMEM((BLK + 1, 7, PB, PB), F32),
            pltpu.VMEM((BLK // 2, PB, 2 * PB), BF16),
            pltpu.VMEM((7 * PB, PB), BF16),
            pltpu.VMEM((3, PB, PB), F32),
            pltpu.VMEM((3, PB, PB), F32),
            pltpu.VMEM((3, PAIRS, PB), F32),
            pltpu.VMEM((3, PAIRS, PB), F32),
            pltpu.VMEM((3, 4 * BLK, PB), F32),
            pltpu.VMEM((3, 3, BLK, PB), F32),
            pltpu.VMEM((BLK, PB), BF16),
            pltpu.VMEM((sectors * CAP, total), BF16),
            pltpu.VMEM((BLK, PB), BF16),
        ] + [
            pltpu.VMEM((count, rows, PB), F32)
            for rows in (5, 3) for count in (part, total, sectors * CAP, sectors * CAP)
        ] + [pltpu.SemaphoreType.DMA((9,))] + [three] * 4 + [pltpu.SemaphoreType.DMA((3, 3))] * 2 + hops,
        compiler_params=pltpu.CompilerParams(collective_id=0, has_side_effects=True, vmem_limit_bytes=32 << 20),
        name="substeps",
    )(*[pltpu.with_memory_space_constraint(a, pltpu.HBM)
        for a in (pairs, slots, home, pos, vel, rad, gas, history)], count)


def hand_over(x, v, r, hist, x_out, v_out, r_out, hist_out, sems):
    copies = [pltpu.make_async_copy(x, x_out, sems.at[0]),
              pltpu.make_async_copy(v, v_out, sems.at[1]),
              pltpu.make_async_copy(r, r_out, sems.at[2])]
    group = PAIRS // 8
    for n in range(8):
        rows = pl.ds(n * group, group)
        copies.append(pltpu.make_async_copy(hist.at[rows], hist_out.at[rows], sems.at[3 + n]))
    for copy in copies:
        copy.start()
    for copy in copies:
        copy.wait()


def results(x, v, r, hist):
    vmem = pl.BlockSpec(memory_space=pltpu.VMEM)
    hbm = pl.BlockSpec(memory_space=pl.ANY)
    return pl.pallas_call(
        hand_over,
        out_shape=tuple(jax.ShapeDtypeStruct(a.shape, F32) for a in (x, v, r, hist)),
        in_specs=[vmem] * 4,
        out_specs=(hbm,) * 4,
        scratch_shapes=[pltpu.SemaphoreType.DMA((11,))],
        compiler_params=pltpu.CompilerParams(vmem_limit_bytes=16 << 20),
        name="results",
    )(x, v, r, hist)


def local(
    positions,
    velocities,
    radius,
    gas_velocity,
    history,
    pair_list,
    history_slot,
    pair_count,
    new_home,
):
    def planes(array):
        return jnp.transpose(array[0, 0], (1, 0, 2))

    place, speed, radii, memory = results(*substeps(
        lax.axis_size("axial"), lax.axis_size("azim"), pair_list[0, 0], history_slot[0], pair_count, new_home[0],
        planes(positions), planes(velocities), radius[0, 0], planes(gas_velocity), history[0, 0]))
    return (
        jnp.transpose(place, (1, 0, 2))[None, None],
        jnp.transpose(speed, (1, 0, 2))[None, None],
        radii[None, None],
        memory[None, None],
    )


def solution(mesh):
    return jax.shard_map(
        local,
        mesh=mesh,
        in_specs=(
            P("axial", "azim", None, None, None),
            P("axial", "azim", None, None, None),
            P("axial", "azim", None, None),
            P("axial", "azim", None, None, None),
            P("axial", "azim", None, None, None, None),
            P("axial", "azim", None, None),
            P("axial", "azim", None),
            P("axial", "azim"),
            P("axial", "azim", None),
        ),
        out_specs=(
            P("axial", "azim", None, None, None),
            P("axial", "azim", None, None, None),
            P("axial", "azim", None, None),
            P("axial", "azim", None, None, None, None),
        ),
        check_vma=False,
    )
```
